128 devices in a mesh: frames: 64 (over z, y, x_lo, core), dp: 2 (over x_hi).
Axes of the slice: x: 4 (x_hi: 2, x_lo: 2; x = x_hi * 2 + x_lo), y: 4, z: 4, core: 2. Of those that a mesh axis runs over, the one named last changes fastest.
Arguments:
- shifted: bfloat16 [2, 256, 16, 16, 640], P('dp', 'frames'), may hold values from -6 to 6
- out_grad: bfloat16 [2, 256, 16, 16, 640], P('dp', 'frames'), may hold values from -6 to 6
- conv_weight: bfloat16 [640, 5760], P('frames'), may hold values from -0.078125 to 0.078125
- norm_gain: float32 [640], replicated, may hold values from 0.5 to 2
- norm_bias: float32 [640], replicated, may hold values from -4 to 4
- shift_fwd: int32 [80], replicated, may hold values from 0 to 639, as said below
- shift_bwd: int32 [80], replicated, may hold values from 0 to 639, as said below
Outputs:
- in_grad: bfloat16 [2, 256, 16, 16, 640], P('dp', 'frames')
- weight_grad: float32 [640, 5760], P('frames')
- gain_grad: float32 [640], replicated
- bias_grad: float32 [640], replicated
The draws below stay inside these ranges and needn't reach their ends.
Inputs may be any that keep to these rules, and one draw needn't show every extreme that they name: `shift_fwd`: 80 distinct channel numbers, none of them in shift_bwd. `shift_bwd`: 80 distinct channel numbers, none of them in shift_fwd.
All inputs are finite; a program needn't handle non-finite values.
Results may differ from the reference program's by a relative error of at most 0.003.
Values may be sent and summed in bfloat16 or wider, within the bound.
A program may use at most 128 MiB of HBM per device.

```python
import math
import jax
import jax.numpy as jnp
from jax import lax

CH = 640
GROUP_CH = 20
TAPS = 9
FOLD = 80
ROWS = 16
COLS = 16
FRAMES = 256
VIDEOS = 2


def shift_channels(key):
    return jax.random.permutation(jax.random.fold_in(key, 17), CH).astype(jnp.int32)


def draw_shift_fwd(key, part):
    return shift_channels(key)[:FOLD]


def draw_shift_bwd(key, part):
    return shift_channels(key)[FOLD:2 * FOLD]


def steps_of(own_key, shape, cuts, low, top_value):
    def one(axis_at, blocks):
        steps = jax.random.uniform(jax.random.fold_in(jax.random.fold_in(own_key, 6), axis_at), (blocks,), jnp.float32, low / len(cuts), top_value / len(cuts))
        return jnp.repeat(jnp.exp(steps), shape[axis_at] // blocks).reshape((-1,) + (1,) * (len(shape) - axis_at - 1))

    factor_of = one(*cuts[0])
    for cut in cuts[1:]:
        factor_of = factor_of * one(*cut)
    return factor_of


def normal_values(own_key, shape, deviation, reach, split=(), kind=jnp.bfloat16):
    values = jax.random.normal(own_key, shape, jnp.float32) * deviation
    if len(split) > 0:
        values = steps_of(own_key, shape, split, -0.22, 0.18) * values
    return jnp.clip(values, min=-reach, max=reach).astype(kind)


def setup_inputs(seed: int = 0) -> dict:
    splits = jax.random.split(jax.random.key(seed), 8)
    return {
        "shifted": normal_values(splits[0], (VIDEOS, FRAMES, ROWS, COLS, CH), 1.0, 6.0, ((0, 2), (1, 64))),
        "out_grad": normal_values(splits[1], (VIDEOS, FRAMES, ROWS, COLS, CH), 1.0, 6.0, ((0, 2), (1, 64))),
        "conv_weight": normal_values(splits[2], (CH, TAPS * CH), (TAPS * CH) ** -0.5, 0.078125, ((0, 64),)),
        "norm_gain": jnp.clip(jnp.exp(jax.random.uniform(splits[3], (CH,), jnp.float32, math.log(0.5), math.log(2.0))), 0.5, 2.0),
        "norm_bias": normal_values(splits[4], (CH,), 1.0, 4.0, (), jnp.float32),
        "shift_fwd": draw_shift_fwd(jax.random.fold_in(splits[7], 71), 0),
        "shift_bwd": draw_shift_bwd(jax.random.fold_in(splits[7], 71), 0),
    }


epsilon = 1e-05

def pad_space(values):
    return jnp.pad(values, ((0, 0), (1, 1), (1, 1), (0, 0)))

def local_grads(shifted, out_grad, conv_weight, norm_gain, norm_bias):
    frame_count, row_count, col_count, channels = shifted.shape
    groups = channels // GROUP_CH
    values = shifted.astype(jnp.float32).reshape(frame_count, row_count * col_count, groups, GROUP_CH)
    center = lax.optimization_barrier(jnp.mean(values, axis=(1, 3), keepdims=True))
    spread = lax.optimization_barrier(jnp.mean(jnp.square(values - center), axis=(1, 3), keepdims=True))
    inverse = lax.rsqrt(spread + epsilon)
    grouped_normed = (values - center) * inverse
    normed = grouped_normed.reshape(frame_count, row_count, col_count, channels)
    before = normed * norm_gain + norm_bias
    activation = jax.nn.silu(before).astype(jnp.bfloat16)
    act_padded = pad_space(activation)
    grad_padded = pad_space(out_grad)
    grad_rows = out_grad.reshape(-1, channels)
    act_grad = jnp.zeros((grad_rows.shape[0], channels), jnp.float32)
    weight_parts = []
    for tap_index in range(9):
        row_off, col_off = divmod(tap_index, 3)
        grad_view = grad_padded[:, 2 - row_off:2 - row_off + row_count, 2 - col_off:2 - col_off + col_count, :].reshape(-1, channels)
        act_grad = act_grad + jnp.dot(grad_view, conv_weight[:, tap_index * channels:(tap_index + 1) * channels], preferred_element_type=jnp.float32)
        act_view = act_padded[:, row_off:row_off + row_count, col_off:col_off + col_count, :].reshape(-1, channels)
        weight_parts.append(lax.dot_general(grad_rows, act_view, (((0,), (0,)), ((), ())), preferred_element_type=jnp.float32))
    weight_grad = jnp.concatenate(weight_parts, axis=1)
    sigmoid_val = jax.nn.sigmoid(before)
    pre_grad = act_grad.reshape(before.shape) * sigmoid_val * (1.0 + before * (1.0 - sigmoid_val))
    gain_part = lax.optimization_barrier(jnp.sum(pre_grad * normed, axis=(0, 1, 2)))
    bias_part = lax.optimization_barrier(jnp.sum(pre_grad, axis=(0, 1, 2)))
    norm_grad = (pre_grad * norm_gain).reshape(values.shape)
    first_mean = lax.optimization_barrier(jnp.mean(norm_grad, axis=(1, 3), keepdims=True))
    second_mean = lax.optimization_barrier(jnp.mean(norm_grad * grouped_normed, axis=(1, 3), keepdims=True))
    shifted_grad = ((norm_grad - first_mean - grouped_normed * second_mean) * inverse).reshape(shifted.shape)
    return (shifted_grad.astype(jnp.bfloat16), weight_grad, gain_part, bias_part)

def reference(shifted, out_grad, conv_weight, norm_gain, norm_bias, shift_fwd, shift_bwd):
    scale = float(VIDEOS * FRAMES * ROWS * COLS) ** (-0.5)
    grads_list = []
    weight_total = jnp.zeros((CH, TAPS * CH), jnp.float32)
    gain_total = jnp.zeros((CH,), jnp.float32)
    bias_total = jnp.zeros((CH,), jnp.float32)
    for video in range(VIDEOS):
        shifted_grad, weight_part, gain_part, bias_part = local_grads(shifted[video], out_grad[video], conv_weight, norm_gain, norm_bias)
        grads_list.append(shifted_grad)
        weight_total = weight_total + weight_part
        gain_total = gain_total + gain_part
        bias_total = bias_total + bias_part
    shifted_grads = jnp.stack(grads_list)
    channel_ids = jnp.arange(CH, dtype=jnp.int32)
    forward_mask = jnp.any(channel_ids[None, :] == shift_fwd[:, None], axis=0)
    backward_mask = jnp.any(channel_ids[None, :] == shift_bwd[:, None], axis=0)
    later = jnp.concatenate([shifted_grads[:, 1:], jnp.zeros_like(shifted_grads[:, :1])], axis=1)
    earlier = jnp.concatenate([jnp.zeros_like(shifted_grads[:, :1]), shifted_grads[:, :-1]], axis=1)
    in_grad = jnp.where(forward_mask, later, jnp.where(backward_mask, earlier, shifted_grads))
    return (in_grad, weight_total * scale, gain_total * scale, bias_total * scale)
```

```python
import jax
import jax.numpy as jnp
from jax import lax
from jax.experimental import pallas as pl
from jax.experimental.pallas import tpu as pltpu
from jax.sharding import PartitionSpec as P

f32, bf16 = jnp.float32, jnp.bfloat16
MESH = pl.DeviceIdType.MESH
EPS = 1e-05
CH, HALF, WIDE = 640, 320, 1024
HIGH = lax.Precision.HIGHEST


def dot(a, b):
    return jnp.dot(a, b, preferred_element_type=f32)


def dot_nt(a, b):
    return lax.dot_general(a, b, (((1,), (1,)), ((), ())), preferred_element_type=f32)


def rows16(v, n):
    return pl.ds(pl.multiple_of(v, 16), n)


def div20(i):
    return (i * 3277) >> 16


def kernel(
    scale,
    x_ref, g_hbm, w_ref, gain_ref, bias_ref, fwd_ref, bwd_ref,
    ig_ref, wg_ref, gb_ref,
    xs, xb, gp, gt, pm, ap, p1, w, y_acc, pre,
    cen, inv, s1, s2, m1, m2,
    s_buf, wgs, xr, z1s, z1r, z2s, z2r, yf, ys, yr, ds_, dr,
    sgp, igs, igr, hs, hr, selm, ar_s, ar_r, ar_c,
    loc_sem, ex_s, ex_r, p1_s, p1_r, zo_s, zo_r, zf_s, zf_r, cr_s, cr_r, yi_s, yi_r,
    x_s, x_r, z1_ss, z1_rs, z2_ss, z2_rs, y_ss, y_rs, d_ss, d_rs, h_ss, h_rs, a_ss, a_rs,
):
    f = lax.axis_index("frames")
    d = lax.axis_index("dp")
    c = f % 2
    xl = (f // 2) % 2
    y = (f // 4) % 4
    z = f // 16
    x = d * 2 + xl
    y0 = y % 2
    y1 = y // 2

    def dev(zz, yy, xx, cc):
        return {"frames": ((zz * 4 + yy) * 2 + xx % 2) * 2 + cc, "dp": xx // 2}

    oc = 1 - c
    zp, zm, zo = (z + 1) % 4, (z + 3) % 4, (z + 2) % 4
    yin = y + 1 - 2 * y0
    ycross = (y + 3 + 2 * y0) % 4
    xin = x + 1 - 2 * xl
    xcross = (x + 3 + 2 * xl) % 4
    xop = (x + 2) % 4
    sib = dev(z, y, x, oc)
    nxt = {"frames": (f + 2) % 64, "dp": d}
    prv = {"frames": (f + 62) % 64, "dp": d}

    def remote(src, dst, ss, rs, to):
        return pltpu.make_async_remote_copy(
            src_ref=src, dst_ref=dst, send_sem=ss, recv_sem=rs, device_id=to, device_id_type=MESH
        )

    barrier = pltpu.get_barrier_semaphore()
    partners = [sib, nxt, prv]
    for yy, xx in ((yin, x), (y, xin), (yin, xin)):
        partners += [dev(z, yy, xx, 0), dev(z, yy, xx, 1)]
    for k in (2, 3):
        yy = (ycross, (y + 2) % 4)[k - 2]
        partners += [dev(z, yy, x, 0), dev(z, yy, x, 1)]
    partners += [dev(z, y, xcross, c), dev(z, y, xop, c)]
    partners += [dev(zp, y, x, c), dev(zm, y, x, c), dev(zo, y, x, c)]
    for to in partners:
        pl.semaphore_signal(barrier, inc=1, device_id=to, device_id_type=MESH)
    pl.semaphore_wait(barrier, len(partners))

    me8 = (y0 * 2 + xl) * 2 + c
    p1c = []
    k = 0
    for yy, xx, dc in ((y, x, 1), (y, xin, 0), (y, xin, 1), (yin, x, 0), (yin, x, 1), (yin, xin, 0), (yin, xin, 1)):
        cc = c + dc - 2 * c * dc
        p1c.append(remote(w_ref.at[cc], p1.at[me8], p1_s.at[k], p1_r.at[k], dev(z, yy, xx, cc)))
        k += 1
    for cp in p1c:
        cp.start()
    interior = (pl.ds(c * 4, 4), pl.ds(16, 256))
    g_local = pltpu.make_async_copy(g_hbm, gp.at[interior], loc_sem.at[0])
    g_remote = remote(g_hbm, gp.at[interior], ex_s.at[0], ex_r.at[0], sib)
    g_local.start()
    p1[me8] = w_ref[c]

    def split(t, _):
        r = rows16(t * 256, 256)
        v = x_ref[r, :].astype(f32)
        xs[0, r, :] = v[:, :HALF].astype(bf16)
        xs[1, r, :] = v[:, HALF:].astype(bf16)
        return 0

    lax.fori_loop(0, 4, split, 0)
    x_remote = remote(xs.at[oc], xb, ex_s.at[1], ex_r.at[1], sib)
    x_remote.start()
    g_remote.start()

    def read_x(t):
        r = rows16((t % 4) * 256, 256)
        mine = xs[c, r, :]
        other = xb[r, :]
        return jnp.where(t // 4 == c, mine, other).astype(f32)

    zero16 = jnp.zeros((16, CH), bf16)
    zero16w = jnp.zeros((16, WIDE), bf16)
    for t in range(8):
        gp[t, 0:16, :] = zero16
        gp[t, 272:288, :] = zero16
        ap[t, 0:16, :] = zero16w
        ap[t, 272:288, :] = zero16w

    oi = lax.broadcasted_iota(jnp.int32, (CH, CH), 0)
    li = lax.broadcasted_iota(jnp.int32, (CH, CH), 1)
    q = (oi >= HALF).astype(jnp.int32)
    rr = oi - HALF * q
    zy = div20(rr)
    src_row = (2 * zy + (q + xl - 2 * q * xl)) * 20 + (rr - 20 * zy)
    pm[...] = (li == src_row).astype(f32).astype(bf16)
    gi = div20(lax.broadcasted_iota(jnp.int32, (HALF, HALF), 0))
    gj = div20(lax.broadcasted_iota(jnp.int32, (HALF, HALF), 1))
    group_mean = jnp.where(gi == gj, 1.0 / 5120.0, 0.0).astype(f32)

    def spread_groups(v):
        return jnp.dot(v, group_mean, preferred_element_type=f32, precision=HIGH)

    mine0 = c == 0
    gain = jnp.where(mine0, gain_ref[:, :HALF], gain_ref[:, HALF:])
    bias = jnp.where(mine0, bias_ref[:, :HALF], bias_ref[:, HALF:])

    def transpose(t):
        gt[:, pl.ds(pl.multiple_of(t * 256, 256), 256)] = dot_nt(pm[...], gp[t, 16:272, :]).astype(bf16)

    g_local.wait()

    def transpose_mine(i, _):
        transpose(c * 4 + i)
        return 0

    lax.fori_loop(0, 4, transpose_mine, 0)

    for cp in p1c:
        cp.wait_recv()
    blk = z * 2 + y1
    oblk = 1 - 2 * y1
    for lb in range(8):
        for a in range(3):
            r = (lb * 3 + a) * 10
            piece = jnp.concatenate([p1[s, r : r + 10, :].astype(f32) for s in range(8)], axis=0)
            w[a, blk, :, lb * 128 : lb * 128 + 128] = piece.astype(bf16)

    def lanes(qq, n=256):
        return pl.ds(pl.multiple_of(qq * 256, 256), n)

    def wsl(b, qq):
        return w.at[:, b, :, lanes(qq)]

    def z_own(k, qq):
        s = wsl(blk, qq)
        return remote(s, s, zo_s.at[k, qq], zo_r.at[k, qq], dev((zp, zm)[k], y, x, c))

    def z_fwd(qq):
        up = qq < 2
        s = wsl((zm if up else zp) * 2 + y1, qq)
        return remote(s, s, zf_s.at[qq], zf_r.at[qq], dev(zp if up else zm, y, x, c))

    zrel = (z, zm, zp, zo)

    def cross(k, h):
        s = wsl(zrel[k] * 2 + y1, 2 * h + 1 - y0)
        return remote(s, s, cr_s.at[k, h], cr_r.at[k, h], dev(z, ycross, x, c))

    def inner(k, h):
        s = wsl(zrel[k] * 2 + 1 - y1, 2 * h + y0)
        return remote(s, s, yi_s.at[k, h], yi_r.at[k, h], dev(z, yin, x, c))

    cross(0, 0).start()
    for qq in (0, 1):
        z_own(0, qq).start()
        z_own(1, qq).start()
    cross(0, 1).start()
    for qq in (2, 3):
        z_own(0, qq).start()
        z_own(1, qq).start()

    def hook_z(h):
        for qq in (2 * h, 2 * h + 1):
            z_own(0, qq).wait_recv()
            z_own(1, qq).wait_recv()
            z_fwd(qq).start()
        cross(1, h).start()
        cross(2, h).start()

    def hook_opp(h):
        z_fwd(2 * h).wait_recv()
        z_fwd(2 * h + 1).wait_recv()
        cross(3, h).start()

    def hook_in(k, h):
        cross(k, h).wait_recv()
        inner(k, h).start()

    x_remote.wait_recv()

    def stat_sum(t, _):
        s1[pl.ds(t, 1), :] = jnp.sum(read_x(t), axis=0, keepdims=True)
        return 0

    lax.fori_loop(0, 8, stat_sum, 0)
    cen[...] = spread_groups(s1[...])

    def stat_sq(t, _):
        v = read_x(t) - cen[pl.ds(t, 1), :]
        s2[pl.ds(t, 1), :] = jnp.sum(v * v, axis=0, keepdims=True)
        return 0

    lax.fori_loop(0, 8, stat_sq, 0)
    inv[...] = lax.rsqrt(spread_groups(s2[...]) + EPS)

    col = lax.broadcasted_iota(jnp.int32, (256, HALF), 0) % 16

    def normed_of(t):
        return (read_x(t) - cen[pl.ds(t, 1), :]) * inv[pl.ds(t, 1), :]

    def forward(t, _):
        before = normed_of(t) * gain + bias
        act = before / (1.0 + jnp.exp(-before))
        left = jnp.where(col == 0, 0.0, pltpu.roll(act, 1, 0))
        right = jnp.where(col == 15, 0.0, pltpu.roll(act, 255, 0))
        cat = jnp.concatenate([left, act, right, jnp.zeros((256, WIDE - 3 * HALF), f32)], axis=1)
        ap[t, 16:272, :] = cat.astype(bf16)
        return 0

    lax.fori_loop(0, 8, forward, 0)
    g_remote.wait_recv()

    def transpose_other(i, _):
        transpose(oc * 4 + i)
        return 0

    lax.fori_loop(0, 4, transpose_other, 0)
    hook_z(0)
    hook_in(0, 0)

    def x_copy(i):
        n = i % 2
        to = xin + n * (xcross - xin)
        return remote(wgs.at[i], xr.at[i], x_s.at[i], x_r.at[i], dev(z, y, to, c))

    def wg_step(i, _):
        a, n = i // 2, i % 2
        cols = pl.ds(pl.multiple_of(n * 512, 512), 512)
        acc = None
        for t in range(8):
            v = dot(gt[:, t * 256 : t * 256 + 256], ap[t, rows16(a * 16, 256), cols])
            acc = v if acc is None else acc + v
        s_buf[i] = acc[:HALF, :]
        wgs[i] = acc[HALF:, :].astype(bf16)
        x_copy(i).start()

        @pl.when(i == 0)
        def _():
            hook_in(0, 1)

        @pl.when(i == 1)
        def _():
            hook_z(1)
            hook_in(1, 0)

        @pl.when(i == 2)
        def _():
            hook_opp(0)
            hook_in(2, 0)

        @pl.when(i == 3)
        def _():
            hook_opp(1)

        @pl.when(i == 4)
        def _():
            hook_in(3, 0)

        @pl.when(i == 5)
        def _():
            hook_in(1, 1)

        return 0

    lax.fori_loop(0, 6, wg_step, 0)

    def z1_copy(i, k):
        return remote(z1s.at[i, k], z1r.at[i, k], z1_ss.at[i, k], z1_rs.at[i, k], dev((zp, zm)[k], y, x, c))

    def z2_copy(i, k):
        return remote(z2s.at[i, k], z2r.at[i, k], z2_ss.at[i, k], z2_rs.at[i, k], dev((zp, zm)[k], y, x, c))

    def y_copy(i, r):
        dy, dc = r // 2, r % 2
        yy, cc = (y + dy) % 4, c + dc - 2 * c * dc
        return remote(ys.at[i, yy * 2 + cc], yr.at[i, r], y_ss.at[i, r], y_rs.at[i, r], dev(z, yy, x, cc))

    def d_copy(i):
        return remote(ds_.at[i], dr.at[i], d_ss.at[i], d_rs.at[i], dev(z, y, xop, c))

    def block(b):
        return rows16(b * 80, 80)

    def stage1(i):
        x_copy(i).wait_recv()
        s_buf[i] = s_buf[i] + xr[i].astype(f32)
        z1s[i, 0] = s_buf[i, block(zo), 0:256].astype(bf16)
        z1s[i, 1] = s_buf[i, block(zo), 256:512].astype(bf16)
        z1_copy(i, 0).start()
        z1_copy(i, 1).start()

    def stage2(i):
        z1_copy(i, 0).wait_recv()
        z2s[i, 0, :, 0:256] = (s_buf[i, block(zp), 0:256] + z1r[i, 0].astype(f32)).astype(bf16)
        z2s[i, 0, :, 256:512] = s_buf[i, block(zp), 256:512].astype(bf16)
        z2_copy(i, 0).start()
        z1_copy(i, 1).wait_recv()
        z2s[i, 1, :, 0:256] = s_buf[i, block(zm), 0:256].astype(bf16)
        z2s[i, 1, :, 256:512] = (s_buf[i, block(zm), 256:512] + z1r[i, 1].astype(f32)).astype(bf16)
        z2_copy(i, 1).start()

    def stage3(i):
        z2_copy(i, 0).wait_recv()
        z2_copy(i, 1).wait_recv()
        total = s_buf[i, block(z), :] + z2r[i, 0].astype(f32) + z2r[i, 1].astype(f32)
        total = jnp.concatenate([total, jnp.zeros((8, 512), f32)], axis=0)
        for k in range(8):
            piece = total[10 * k : 10 * k + 16, :]
            yf[i, k] = piece
            ys[i, k] = piece.astype(bf16)
        for r in range(1, 8):
            y_copy(i, r).start()

    def stage4(i):
        for r in range(1, 8):
            y_copy(i, r).wait_recv()
        own = yf[i, y * 2 + c]
        for dy in (1, 2, 3):
            own = own + yr[i, 2 * dy].astype(f32)
        other = yr[i, 1].astype(f32)
        for dy in (1, 2, 3):
            other = other + yr[i, 2 * dy + 1].astype(f32)
        ds_[i, 0] = own
        ds_[i, 1] = other
        d_copy(i).start()

    def stage5(i):
        d_copy(i).wait_recv()
        own = (ds_[i, 0] + dr[i, 0]) * scale
        other = (ds_[i, 1] + dr[i, 1]) * scale
        a, n = i // 2, i % 2
        cols = pl.ds(pl.multiple_of(n * 512, 512), 512)
        wg_ref[0, a, :, cols] = jnp.where(mine0, own, other)
        wg_ref[1, a, :, cols] = jnp.where(mine0, other, own)

    stages = (stage1, stage2, stage3, stage4, stage5)

    def rs_slot(s):
        for k in range(5):
            i = s - k

            @pl.when(jnp.logical_and(i >= 0, i < 6))
            def _(k=k, i=i):
                stages[k](i)

    hook_in(2, 1)
    for k in range(4):
        inner(k, 0).wait_recv()

    def act_step(i, _):
        n, tt = i // 4, i % 4

        @pl.when(i == 0)
        def _():
            hook_in(3, 1)

        @pl.when(i == 4)
        def _():
            for k in range(4):
                inner(k, 1).wait_recv()

        cols = pl.ds(pl.multiple_of(n * 512, 512), 512)
        lhs = jnp.concatenate(
            [
                jnp.concatenate([gp[tt * 2 + t, 16 * (2 - a) : 16 * (2 - a) + 256, :] for a in range(3)], axis=1)
                for t in range(2)
            ],
            axis=0,
        )
        rhs = w[:, :, :, cols].reshape(3 * CH, 512)
        y_acc[rows16(tt * 512, 512), cols] = dot(lhs, rhs)
        rs_slot(i)
        return 0

    lax.fori_loop(0, 8, act_step, 0)

    def back1(t, _):
        r = rows16(t * 256, 256)
        v = y_acc[r, :]
        right = jnp.where(col == 15, 0.0, pltpu.roll(v[:, :HALF], 255, 0))
        left = jnp.where(col == 0, 0.0, pltpu.roll(v[:, 2 * HALF : 3 * HALF], 1, 0))
        act_grad = right + v[:, HALF : 2 * HALF] + left
        normed = normed_of(t)
        before = normed * gain + bias
        g = 1.0 / (1.0 + jnp.exp(-before))
        p = act_grad * g * (1.0 + before * (1.0 - g))
        pre[r, :] = p
        s1[pl.ds(t, 1), :] = jnp.sum(p * normed, axis=0, keepdims=True)
        s2[pl.ds(t, 1), :] = jnp.sum(p, axis=0, keepdims=True)
        return 0

    lax.fori_loop(0, 8, back1, 0)
    m1[...] = spread_groups(s2[...] * gain)
    m2[...] = spread_groups(s1[...] * gain)

    own_sum = jnp.concatenate(
        [jnp.sum(s1[...], axis=0, keepdims=True), jnp.sum(s2[...], axis=0, keepdims=True), jnp.zeros((6, HALF), f32)],
        axis=0,
    )

    def ar_copy(st, k):
        to = (
            (dev(z, y, xin, c), dev(z, y, xcross, c), dev(z, y, xop, c)),
            (dev(z, yin, x, c), dev(z, ycross, x, c), dev(z, (y + 2) % 4, x, c)),
            (dev(zp, y, x, c), dev(zm, y, x, c), dev(zo, y, x, c)),
        )[st][k]
        return remote(ar_s.at[st], ar_r.at[st, k], a_ss.at[st, k], a_rs.at[st, k], to)

    def ar_send(st, v):
        ar_s[st] = v
        for k in range(3):
            ar_copy(st, k).start()

    def ar_sum(st):
        v = ar_s[st]
        for k in range(3):
            ar_copy(st, k).wait_recv()
        return v + ar_r[st, 0] + ar_r[st, 1] + ar_r[st, 2]

    ar_send(0, own_sum)

    def back2(t, _):
        r = rows16(t * 256, 256)
        v = pre[r, :] * gain - m1[pl.ds(t, 1), :] - normed_of(t) * m2[pl.ds(t, 1), :]
        sgp[t + 1] = (v * inv[pl.ds(t, 1), :]).astype(bf16)
        return 0

    back2(0, 0)
    back2(7, 0)

    ch_id = lax.broadcasted_iota(jnp.int32, (HALF, 128), 0) + c * HALF
    selm[0] = (ch_id == bwd_ref[...]).astype(f32).astype(bf16)
    selm[1] = (ch_id == fwd_ref[...]).astype(f32).astype(bf16)
    hs[0] = dot(sgp[8], selm[0]).astype(bf16)
    hs[1] = dot(sgp[1], selm[1]).astype(bf16)
    halo = [
        remote(hs.at[0], hr.at[0], h_ss.at[0], h_rs.at[0], nxt),
        remote(hs.at[1], hr.at[1], h_ss.at[1], h_rs.at[1], prv),
    ]
    halo[0].start()
    halo[1].start()
    ones = jnp.ones((8, 128), bf16)
    bwd_mask = dot_nt(ones, selm[0])[0:1, :] > 0.5
    fwd_mask = dot_nt(ones, selm[1])[0:1, :] > 0.5

    rs_slot(8)
    lax.fori_loop(1, 7, back2, 0)
    ar_send(1, ar_sum(0))
    rs_slot(9)
    halo[0].wait_recv()
    halo[1].wait_recv()
    keep_prev = jnp.where(f >= 2, 1.0, 0.0)
    keep_next = jnp.where(f < 62, 1.0, 0.0)
    sgp[0] = (dot_nt(hr[0], selm[0]) * keep_prev).astype(bf16)
    sgp[9] = (dot_nt(hr[1], selm[1]) * keep_next).astype(bf16)

    def shift(t):
        v = jnp.where(bwd_mask, sgp[t].astype(f32), sgp[t + 1].astype(f32))
        return jnp.where(fwd_mask, sgp[t + 2].astype(f32), v)

    def shift_other(i, _):
        igs[i] = shift(oc * 4 + i).astype(bf16)
        return 0

    lax.fori_loop(0, 4, shift_other, 0)
    i_copy = remote(igs, igr, ex_s.at[2], ex_r.at[2], sib)
    i_copy.start()
    ar_send(2, ar_sum(1))
    rs_slot(10)
    total = ar_sum(2)
    ar_c[0] = total
    c_copy = remote(ar_c.at[0], ar_c.at[1], ex_s.at[3], ex_r.at[3], sib)
    c_copy.start()
    i_copy.wait_recv()

    def assemble(i, _):
        own = shift(c * 4 + i)
        other = igr[i].astype(f32)
        v = jnp.concatenate([jnp.where(mine0, own, other), jnp.where(mine0, other, own)], axis=1)
        ig_ref[rows16(i * 256, 256), :] = v.astype(bf16)
        return 0

    lax.fori_loop(0, 4, assemble, 0)
    c_copy.wait_recv()
    own = ar_c[0] * scale
    other = ar_c[1] * scale
    gb_ref[0] = jnp.where(mine0, own, other)
    gb_ref[1] = jnp.where(mine0, other, own)

    for cp in p1c:
        cp.wait_send()
    for cp in (g_remote, x_remote, i_copy, c_copy, halo[0], halo[1]):
        cp.wait_send()
    for qq in range(4):
        z_own(0, qq).wait_send()
        z_own(1, qq).wait_send()
        z_fwd(qq).wait_send()
    for k in range(4):
        for h in range(2):
            cross(k, h).wait_send()
            inner(k, h).wait_send()
    for st in range(3):
        for k in range(3):
            ar_copy(st, k).wait_send()

    def drain(i, _):
        x_copy(i).wait_send()
        for k in range(2):
            z1_copy(i, k).wait_send()
            z2_copy(i, k).wait_send()
        for r in range(1, 8):
            y_copy(i, r).wait_send()
        d_copy(i).wait_send()
        return 0

    lax.fori_loop(0, 6, drain, 0)


def on_device(shifted, out_grad, conv_weight, norm_gain, norm_bias, shift_fwd, shift_bwd):
    scale = 131072.0 ** (-0.5)
    x = shifted.reshape(1024, CH)
    g = out_grad.reshape(4, 256, CH)
    wp = conv_weight.reshape(10, 3, 3, 2, HALF).transpose(3, 1, 0, 2, 4).reshape(2, 3, 10, 3 * HALF)
    wp = jnp.pad(wp, ((0, 0), (0, 0), (0, 0), (0, WIDE - 3 * HALF)))
    wp = wp.reshape(2, 3, 10, 8, 128).transpose(0, 3, 1, 2, 4).reshape(2, 240, 128)
    pad = lambda v: jnp.pad(v, (0, 48), constant_values=-1).reshape(1, 128)
    dma = pltpu.SemaphoreType.DMA
    vm = pltpu.VMEM
    scratch = [
        vm((2, 1024, HALF), bf16), vm((1024, HALF), bf16), vm((8, 288, CH), bf16), vm((CH, 2048), bf16),
        vm((CH, CH), bf16), vm((8, 288, WIDE), bf16), vm((8, 240, 128), bf16), vm((3, 8, 80, WIDE), bf16),
        vm((2048, WIDE), f32), vm((2048, HALF), f32),
        vm((8, HALF), f32), vm((8, HALF), f32), vm((8, HALF), f32), vm((8, HALF), f32), vm((8, HALF), f32), vm((8, HALF), f32),
        vm((6, HALF, 512), f32), vm((6, HALF, 512), bf16), vm((6, HALF, 512), bf16),
        vm((6, 2, 80, 256), bf16), vm((6, 2, 80, 256), bf16), vm((6, 2, 80, 512), bf16), vm((6, 2, 80, 512), bf16),
        vm((6, 8, 16, 512), f32), vm((6, 8, 16, 512), bf16), vm((6, 8, 16, 512), bf16),
        vm((6, 2, 16, 512), f32), vm((6, 2, 16, 512), f32),
        vm((10, 256, HALF), bf16), vm((4, 256, HALF), bf16), vm((4, 256, HALF), bf16),
        vm((2, 256, 128), bf16), vm((2, 256, 128), bf16), vm((2, HALF, 128), bf16),
        vm((3, 8, HALF), f32), vm((3, 3, 8, HALF), f32), vm((2, 8, HALF), f32),
        dma((1,)), dma((4,)), dma((4,)), dma((7,)), dma((7,)), dma((2, 4)), dma((2, 4)), dma((4,)), dma((4,)),
        dma((4, 2)), dma((4, 2)), dma((4, 2)), dma((4, 2)),
        dma((6,)), dma((6,)), dma((6, 2)), dma((6, 2)), dma((6, 2)), dma((6, 2)), dma((6, 8)), dma((6, 8)),
        dma((6,)), dma((6,)), dma((2,)), dma((2,)), dma((3, 3)), dma((3, 3)),
    ]
    v = pl.BlockSpec(memory_space=pltpu.VMEM)

    def body(*refs):
        kernel(scale, *refs)

    ig, wg, gb = pl.pallas_call(
        body,
        out_shape=(
            jax.ShapeDtypeStruct((1024, CH), bf16),
            jax.ShapeDtypeStruct((2, 3, 16, WIDE), f32),
            jax.ShapeDtypeStruct((2, 8, HALF), f32),
        ),
        in_specs=[v, pl.BlockSpec(memory_space=pl.ANY), v, v, v, v, v],
        out_specs=(v, v, v),
        scratch_shapes=scratch,
        compiler_params=pltpu.CompilerParams(collective_id=0, has_side_effects=True, vmem_limit_bytes=60 << 20),
    )(x, g, wp, norm_gain.reshape(1, CH), norm_bias.reshape(1, CH), pad(shift_fwd), pad(shift_bwd))
    wg = wg[:, :, :10, : 3 * HALF].reshape(2, 3, 10, 3, HALF).transpose(2, 1, 3, 0, 4).reshape(10, 9 * CH)
    return (ig.reshape(shifted.shape), wg, gb[:, 0].reshape(CH), gb[:, 1].reshape(CH))


def solution(mesh):
    in_specs = (
        P("dp", "frames", None, None, None),
        P("dp", "frames", None, None, None),
        P("frames", None),
        P(),
        P(),
        P(),
        P(),
    )
    out_specs = (P("dp", "frames", None, None, None), P("frames", None), P(), P())
    return jax.shard_map(
        on_device, mesh=mesh, in_specs=in_specs, out_specs=out_specs, check_vma=False
    )
```

```python
import jax
import jax.numpy as jnp
from jax import lax
from jax.experimental import pallas as pl
from jax.experimental.pallas import tpu as pltpu
from jax.sharding import PartitionSpec as P

f32, bf16 = jnp.float32, jnp.bfloat16
MESH = pl.DeviceIdType.MESH
EPS = 1e-05
CH, HALF, WIDE = 640, 320, 1024
HIGH = lax.Precision.HIGHEST


def dot(a, b):
    return jnp.dot(a, b, preferred_element_type=f32)


def dot_nt(a, b):
    return lax.dot_general(a, b, (((1,), (1,)), ((), ())), preferred_element_type=f32)


def rows16(v, n):
    return pl.ds(pl.multiple_of(v, 16), n)


def div20(i):
    return (i * 3277) >> 16


def kernel(
    scale,
    x_hbm, g_hbm, w_ref, gain_ref, bias_ref, fwd_ref, bwd_ref,
    ig_ref, fin, gb_ref,
    wpc, x_ref, xs, xb, gp, gt, pm, ap, p1, w, y_acc, pre,
    cen, inv, s1, s2, m1, m2,
    s_buf, wgs, xr, zs, zr, yf, ys, yr, ds_, dr,
    sgp, igs, igr, hs, hr, selm, a1s, a1r, a2s, a2r,
    loc_sem, ex_s, ex_r, p1_s, p1_r, zo_s, zo_r, zf_s, zf_r, cr_s, cr_r, yi_s, yi_r,
    x_s, x_r, z_ss, z_rs, y_ss, y_rs, d_ss, d_rs, h_ss, h_rs, a1_ss, a1_rs, a2_ss, a2_rs,
):
    f = lax.axis_index("frames")
    d = lax.axis_index("dp")
    c = f % 2
    xl = (f // 2) % 2
    y = (f // 4) % 4
    z = f // 16
    x = d * 2 + xl
    y0 = y % 2
    y1 = y // 2

    def dev(zz, yy, xx, cc):
        return {"frames": ((zz * 4 + yy) * 2 + xx % 2) * 2 + cc, "dp": xx // 2}

    oc = 1 - c
    zp, zm, zo = (z + 1) % 4, (z + 3) % 4, (z + 2) % 4
    yin = y + 1 - 2 * y0
    ycross = (y + 3 + 2 * y0) % 4
    xin = x + 1 - 2 * xl
    xcross = (x + 3 + 2 * xl) % 4
    xop = (x + 2) % 4
    sib = dev(z, y, x, oc)
    nxt = {"frames": (f + 2) % 64, "dp": d}
    prv = {"frames": (f + 62) % 64, "dp": d}

    def remote(src, dst, ss, rs, to):
        return pltpu.make_async_remote_copy(
            src_ref=src, dst_ref=dst, send_sem=ss, recv_sem=rs, device_id=to, device_id_type=MESH
        )

    barrier = pltpu.get_barrier_semaphore()
    partners = [sib, nxt, prv]
    for yy, xx in ((yin, x), (y, xin), (yin, xin)):
        partners += [dev(z, yy, xx, 0), dev(z, yy, xx, 1)]
    for k in (2, 3):
        yy = (ycross, (y + 2) % 4)[k - 2]
        partners += [dev(z, yy, x, 0), dev(z, yy, x, 1)]
    for xx in (xcross, xop):
        partners += [dev(z, y, xx, 0), dev(z, y, xx, 1)]
    partners += [dev(zz, (y + dy) % 4, x, c) for zz in (zp, zm, zo) for dy in range(4)]
    for to in partners:
        pl.semaphore_signal(barrier, inc=1, device_id=to, device_id_type=MESH)

    x_local = pltpu.make_async_copy(x_hbm, x_ref, loc_sem.at[1])
    x_local.start()
    for h in range(2):
        wide = []
        for a in range(3):
            taps = [w_ref[:, (3 * a + b) * CH + h * HALF : (3 * a + b) * CH + (h + 1) * HALF].astype(f32) for b in range(3)]
            wide.append(jnp.concatenate(taps + [jnp.zeros((10, WIDE - 3 * HALF), f32)], axis=1))
        pieces = [wide[a][:, lb * 128 : lb * 128 + 128] for lb in range(8) for a in range(3)]
        wpc[h] = jnp.concatenate(pieces, axis=0).astype(bf16)
    pl.semaphore_wait(barrier, len(partners))
    me8 = (y0 * 2 + xl) * 2 + c
    p1c = []
    k = 0
    for yy, xx, dc in ((y, x, 1), (y, xin, 0), (y, xin, 1), (yin, x, 0), (yin, x, 1), (yin, xin, 0), (yin, xin, 1)):
        cc = c + dc - 2 * c * dc
        p1c.append(remote(wpc.at[cc], p1.at[me8], p1_s.at[k], p1_r.at[k], dev(z, yy, xx, cc)))
        k += 1
    for cp in p1c:
        cp.start()
    interior = (pl.ds(c * 4, 4), pl.ds(16, 256))
    g_local = pltpu.make_async_copy(g_hbm, gp.at[interior], loc_sem.at[0])
    g_remote = remote(g_hbm, gp.at[interior], ex_s.at[0], ex_r.at[0], sib)
    g_local.start()
    p1[me8] = wpc[c]

    x_local.wait()
    def split(t, _):
        r = rows16(t * 256, 256)
        v = x_ref[r, :].astype(f32)
        xs[0, r, :] = v[:, :HALF].astype(bf16)
        xs[1, r, :] = v[:, HALF:].astype(bf16)
        return 0

    lax.fori_loop(0, 4, split, 0)
    x_remote = remote(xs.at[oc], xb, ex_s.at[1], ex_r.at[1], sib)
    x_remote.start()
    g_remote.start()

    def read_x(t):
        r = rows16((t % 4) * 256, 256)
        mine = xs[c, r, :]
        other = xb[r, :]
        return jnp.where(t // 4 == c, mine, other).astype(f32)

    zero16 = jnp.zeros((16, CH), bf16)
    zero16w = jnp.zeros((16, WIDE), bf16)
    for t in range(8):
        gp[t, 0:16, :] = zero16
        gp[t, 272:288, :] = zero16
        ap[t, 0:16, :] = zero16w
        ap[t, 272:288, :] = zero16w

    oi = lax.broadcasted_iota(jnp.int32, (CH, CH), 0)
    li = lax.broadcasted_iota(jnp.int32, (CH, CH), 1)
    q = (oi >= HALF).astype(jnp.int32)
    rr = oi - HALF * q
    zy = div20(rr)
    src_row = (2 * zy + (q + xl - 2 * q * xl)) * 20 + (rr - 20 * zy)
    pm[...] = (li == src_row).astype(f32).astype(bf16)
    gi = div20(lax.broadcasted_iota(jnp.int32, (HALF, HALF), 0))
    gj = div20(lax.broadcasted_iota(jnp.int32, (HALF, HALF), 1))
    group_mean = jnp.where(gi == gj, 1.0 / 5120.0, 0.0).astype(f32)

    def spread_groups(v):
        return jnp.dot(v, group_mean, preferred_element_type=f32, precision=HIGH)

    mine0 = c == 0
    gain_all, bias_all = gain_ref[...].reshape(1, CH), bias_ref[...].reshape(1, CH)
    gain = jnp.where(mine0, gain_all[:, :HALF], gain_all[:, HALF:])
    bias = jnp.where(mine0, bias_all[:, :HALF], bias_all[:, HALF:])

    def transpose(t):
        gt[:, pl.ds(pl.multiple_of(t * 256, 256), 256)] = dot_nt(pm[...], gp[t, 16:272, :]).astype(bf16)

    g_local.wait()

    def transpose_mine(i, _):
        transpose(c * 4 + i)
        return 0

    lax.fori_loop(0, 4, transpose_mine, 0)

    for cp in p1c:
        cp.wait_recv()
    blk = z * 2 + y1
    oblk = 1 - 2 * y1
    for lb in range(8):
        for a in range(3):
            r = (lb * 3 + a) * 10
            piece = jnp.concatenate([p1[s, r : r + 10, :].astype(f32) for s in range(8)], axis=0)
            w[a, blk, :, lb * 128 : lb * 128 + 128] = piece.astype(bf16)

    def lanes(qq, n=256):
        return pl.ds(pl.multiple_of(qq * 256, 256), n)

    def wsl(b, qq):
        return w.at[:, b, :, lanes(qq)]

    def quarter(j):
        return (2 * (j % 2) + 1 - y0) if j < 2 else (2 * (j % 2) + y0)

    def z_own(k, j):
        s = wsl(blk, quarter(j))
        return remote(s, s, zo_s.at[k, j], zo_r.at[k, j], dev((zp, zm)[k], y, x, c))

    def z_fwd(j):
        up = j % 2 == 0
        s = wsl((zm if up else zp) * 2 + y1, quarter(j))
        return remote(s, s, zf_s.at[j], zf_r.at[j], dev(zp if up else zm, y, x, c))

    zrel = (z, zm, zp, zo)

    def cross(k, h):
        s = wsl(zrel[k] * 2 + y1, 2 * h + 1 - y0)
        return remote(s, s, cr_s.at[k, h], cr_r.at[k, h], dev(z, ycross, x, c))

    def inner(k, h):
        s = wsl(zrel[k] * 2 + 1 - y1, 2 * h + y0)
        return remote(s, s, yi_s.at[k, h], yi_r.at[k, h], dev(z, yin, x, c))

    def z_start(j):
        z_own(0, j).start()
        z_own(1, j).start()

    def z_wait(j):
        z_own(0, j).wait_recv()
        z_own(1, j).wait_recv()

    def hook_in(k, h):
        cross(k, h).wait_recv()
        inner(k, h).start()

    def hook0():
        z_start(1)
        cross(0, 1).start()

    def hook1():
        z_wait(0)
        z_fwd(0).start()
        cross(1, 0).start()
        hook_in(0, 0)

    def hook2():
        cross(2, 0).start()
        z_start(2)

    def hook3():
        z_wait(1)
        z_fwd(1).start()
        cross(1, 1).start()
        hook_in(0, 1)

    def hook4():
        z_fwd(0).wait_recv()
        cross(3, 0).start()
        hook_in(1, 0)
        z_start(3)

    def hook5():
        hook_in(2, 0)
        cross(2, 1).start()

    def hook6():
        z_wait(2)
        z_fwd(2).start()
        z_fwd(1).wait_recv()
        cross(3, 1).start()

    def hook7():
        hook_in(3, 0)
        z_wait(3)
        z_fwd(3).start()

    def hook8():
        hook_in(1, 1)

    cross(0, 0).start()
    z_start(0)

    x_remote.wait_recv()

    def stat_sum(t, _):
        s1[pl.ds(t, 1), :] = jnp.sum(read_x(t), axis=0, keepdims=True)
        return 0

    lax.fori_loop(0, 8, stat_sum, 0)
    cen[...] = spread_groups(s1[...])

    def stat_sq(t, _):
        v = read_x(t) - cen[pl.ds(t, 1), :]
        s2[pl.ds(t, 1), :] = jnp.sum(v * v, axis=0, keepdims=True)
        return 0

    lax.fori_loop(0, 8, stat_sq, 0)
    inv[...] = lax.rsqrt(spread_groups(s2[...]) + EPS)

    col = lax.broadcasted_iota(jnp.int32, (256, HALF), 0) % 16

    def normed_of(t):
        return (read_x(t) - cen[pl.ds(t, 1), :]) * inv[pl.ds(t, 1), :]

    def forward(t, _):
        before = normed_of(t) * gain + bias
        act = before / (1.0 + jnp.exp(-before))
        left = jnp.where(col == 0, 0.0, pltpu.roll(act, 1, 0))
        right = jnp.where(col == 15, 0.0, pltpu.roll(act, 255, 0))
        cat = jnp.concatenate([left, act, right, jnp.zeros((256, WIDE - 3 * HALF), f32)], axis=1)
        ap[t, 16:272, :] = cat.astype(bf16)
        return 0

    lax.fori_loop(0, 2, forward, 0)
    hook0()
    lax.fori_loop(2, 8, forward, 0)
    hook1()
    g_remote.wait_recv()

    def transpose_other(i, _):
        transpose(oc * 4 + i)
        return 0

    lax.fori_loop(0, 4, transpose_other, 0)
    hook2()

    def x_copy(i, k):
        to = (xin, xcross)[k]
        return remote(wgs.at[i, k], xr.at[i, k], x_s.at[i, k], x_r.at[i, k], dev(z, y, to, c))

    def wg_step(i, _):
        a, n = i // 2, i % 2
        cols = pl.ds(pl.multiple_of(n * 512, 512), 512)
        acc = None
        for t in range(8):
            v = dot(gt[:, t * 256 : t * 256 + 256], ap[t, rows16(a * 16, 256), cols])
            acc = v if acc is None else acc + v
        s_buf[i] = acc[:HALF, :]
        wgs[i, 0] = acc[HALF:, :256].astype(bf16)
        wgs[i, 1] = acc[HALF:, 256:].astype(bf16)
        x_copy(i, 0).start()
        x_copy(i, 1).start()

        for k, hook in enumerate((hook3, hook4, hook5, hook6, hook7, hook8)):
            pl.when(i == k)(hook)
        pl.when(i == 4)(lambda: stage1(0))
        return 0

    def z_copy(i, k):
        return remote(zs.at[i, k], zr.at[i, k], z_ss.at[i, k], z_rs.at[i, k], dev((zp, zm, zo)[k], y, x, c))

    def y_copy(i, r):
        dy, dc = r // 2, r % 2
        yy, cc = (y + dy) % 4, c + dc - 2 * c * dc
        return remote(ys.at[i, yy * 2 + cc], yr.at[i, r], y_ss.at[i, r], y_rs.at[i, r], dev(z, yy, x, cc))

    def d_copy(i):
        return remote(ds_.at[i], dr.at[i], d_ss.at[i], d_rs.at[i], dev(z, y, xop, c))

    def block(b):
        return rows16(b * 80, 80)

    def stage1(i):
        x_copy(i, 0).wait_recv()
        x_copy(i, 1).wait_recv()
        s_buf[i, :, :256] = s_buf[i, :, :256] + xr[i, 0].astype(f32)
        s_buf[i, :, 256:] = s_buf[i, :, 256:] + xr[i, 1].astype(f32)
        for k in range(3):
            zs[i, k] = s_buf[i, block((zp, zm, zo)[k]), :].astype(bf16)
            z_copy(i, k).start()

    def stage2(i):
        total = s_buf[i, block(z), :]
        for k in range(3):
            z_copy(i, k).wait_recv()
            total = total + zr[i, k].astype(f32)
        total = jnp.concatenate([total, jnp.zeros((8, 512), f32)], axis=0)
        for k in range(8):
            piece = total[10 * k : 10 * k + 16, :]
            yf[i, k] = piece
            ys[i, k] = piece.astype(bf16)
        for r in range(1, 8):
            y_copy(i, r).start()

    def stage3(i):
        for r in range(1, 8):
            y_copy(i, r).wait_recv()
        own = yf[i, y * 2 + c]
        for dy in (1, 2, 3):
            own = own + yr[i, 2 * dy].astype(f32)
        other = yr[i, 1].astype(f32)
        for dy in (1, 2, 3):
            other = other + yr[i, 2 * dy + 1].astype(f32)
        ds_[i, 0] = own
        ds_[i, 1] = other
        d_copy(i).start()

    def stage4(i):
        d_copy(i).wait_recv()
        own = (ds_[i, 0] + dr[i, 0]) * scale
        other = (ds_[i, 1] + dr[i, 1]) * scale
        a, n = i // 2, i % 2
        cols = pl.ds(pl.multiple_of(n * 512, 512), 512)
        fin[0, a, :, cols] = jnp.where(mine0, own, other)
        fin[1, a, :, cols] = jnp.where(mine0, other, own)

    lax.fori_loop(0, 6, wg_step, 0)
    stage1(1)
    for k in range(4):
        inner(k, 0).wait_recv()
    z_fwd(2).wait_recv()

    def back1(t, _):
        r = rows16(t * 256, 256)
        v = y_acc[r, :]
        right = jnp.where(col == 15, 0.0, pltpu.roll(v[:, :HALF], 255, 0))
        left = jnp.where(col == 0, 0.0, pltpu.roll(v[:, 2 * HALF : 3 * HALF], 1, 0))
        act_grad = right + v[:, HALF : 2 * HALF] + left
        normed = normed_of(t)
        before = normed * gain + bias
        g = 1.0 / (1.0 + jnp.exp(-before))
        p = act_grad * g * (1.0 + before * (1.0 - g))
        pre[r, :] = p
        s1[pl.ds(t, 1), :] = jnp.sum(p * normed, axis=0, keepdims=True)
        s2[pl.ds(t, 1), :] = jnp.sum(p, axis=0, keepdims=True)
        return 0

    def back2(t, _):
        r = rows16(t * 256, 256)
        v = pre[r, :] * gain - m1[pl.ds(t, 1), :] - normed_of(t) * m2[pl.ds(t, 1), :]
        sgp[t + 1] = (v * inv[pl.ds(t, 1), :]).astype(bf16)
        return 0

    def back1_of(frames):
        for t in frames:
            back1(t, 0)

    def group_terms():
        m1[...] = spread_groups(s2[...] * gain)
        m2[...] = spread_groups(s1[...] * gain)

    halo = [
        remote(hs.at[0], hr.at[0], h_ss.at[0], h_rs.at[0], nxt),
        remote(hs.at[1], hr.at[1], h_ss.at[1], h_rs.at[1], prv),
    ]
    ch_id = lax.broadcasted_iota(jnp.int32, (HALF, 80), 0) + c * HALF
    selm[0] = (ch_id == bwd_ref[...].reshape(1, 80)).astype(f32).astype(bf16)
    selm[1] = (ch_id == fwd_ref[...].reshape(1, 80)).astype(f32).astype(bf16)

    def edge_frames():
        back1_of((0, 1, 6, 7))
        group_terms()
        back2(0, 0)
        back2(7, 0)
        hs[0] = dot(sgp[8], selm[0]).astype(bf16)
        hs[1] = dot(sgp[1], selm[1]).astype(bf16)
        halo[0].start()
        halo[1].start()

    def act_step(i, _):
        n = i // 4
        tt = (i + 3 * n) % 4

        @pl.when(i == 4)
        def _():
            for k in range(4):
                inner(k, 1).wait_recv()
            z_fwd(3).wait_recv()

        cols = pl.ds(pl.multiple_of(n * 512, 512), 512)
        lhs = jnp.concatenate(
            [
                jnp.concatenate([gp[tt * 2 + t, 16 * (2 - a) : 16 * (2 - a) + 256, :] for a in range(3)], axis=1)
                for t in range(2)
            ],
            axis=0,
        )
        rhs = w[:, :, :, cols].reshape(3 * CH, 512)
        y_acc[rows16(tt * 512, 512), cols] = dot(lhs, rhs)
        plan = {
            0: [(stage1, 2)],
            1: [],
            2: [(stage2, 0), (stage1, 3)],
            3: [(stage2, 1)],
            4: [(stage1, 4)],
            5: [(stage3, 0), (stage2, 2), (stage1, 5)],
            6: [(stage3, 1), (stage2, 3)],
            7: [(stage3, 2), (stage2, 4)],
        }
        for k, work in plan.items():

            @pl.when(i == k)
            def _(k=k, work=work):
                if k < 2:
                    hook_in(k + 2, 1)
                for stage, chunk in work:
                    stage(chunk)

        pl.when(i == 5)(edge_frames)
        return 0

    lax.fori_loop(0, 8, act_step, 0)

    def a1_copy(r):
        dx, dc = r // 2, r % 2
        cc = c + dc - 2 * c * dc
        return remote(a1s, a1r.at[r], a1_ss.at[r], a1_rs.at[r], dev(z, y, (x + dx) % 4, cc))

    def a2_copy(r):
        return remote(a2s, a2r.at[r], a2_ss.at[r], a2_rs.at[r], dev((z + r // 4) % 4, (y + r % 4) % 4, x, c))

    back1_of((2, 3, 4, 5))
    total = [jnp.sum(v[...], axis=0, keepdims=True) for v in (s1, s2)]
    a1s[...] = jnp.concatenate(total + [jnp.zeros((6, HALF), f32)], axis=0)
    for r in range(1, 8):
        a1_copy(r).start()
    stage2(5)
    group_terms()
    lax.fori_loop(1, 7, back2, 0)
    stage3(3)
    halo[0].wait_recv()
    halo[1].wait_recv()
    keep_prev = jnp.where(f >= 2, 1.0, 0.0)
    keep_next = jnp.where(f < 62, 1.0, 0.0)
    sgp[0] = (dot_nt(hr[0], selm[0]) * keep_prev).astype(bf16)
    sgp[9] = (dot_nt(hr[1], selm[1]) * keep_next).astype(bf16)
    ones = jnp.ones((8, 80), bf16)
    bwd_mask = dot_nt(ones, selm[0])[0:1, :] > 0.5
    fwd_mask = dot_nt(ones, selm[1])[0:1, :] > 0.5

    def shift(t):
        v = jnp.where(bwd_mask, sgp[t].astype(f32), sgp[t + 1].astype(f32))
        return jnp.where(fwd_mask, sgp[t + 2].astype(f32), v)

    def shift_other(i, _):
        igs[i] = shift(oc * 4 + i).astype(bf16)
        return 0

    lax.fori_loop(0, 4, shift_other, 0)
    i_copy = remote(igs, igr, ex_s.at[2], ex_r.at[2], sib)
    i_copy.start()
    stage3(4)
    for r in range(1, 8):
        a1_copy(r).wait_recv()
    own = a1s[0:2, :]
    for r in (2, 4, 6):
        own = own + a1r[r, 0:2, :]
    other = a1r[1, 0:2, :]
    for r in (3, 5, 7):
        other = other + a1r[r, 0:2, :]
    a2s[...] = jnp.concatenate([own, other, jnp.zeros((4, HALF), f32)], axis=0)
    for r in range(1, 16):
        a2_copy(r).start()
    stage3(5)

    def keep(i, _):
        ig_ref[c, rows16(i * 256, 256), :] = shift(c * 4 + i).astype(bf16)
        return 0

    lax.fori_loop(0, 4, keep, 0)
    i_copy.wait_recv()
    ig_ref[oc] = igr[...].reshape(1024, HALF)
    for i in range(5):
        stage4(i)
    total = a2s[...]
    for r in range(1, 16):
        a2_copy(r).wait_recv()
        total = total + a2r[r]
    total = total * scale
    gb_ref[c, 0:2, :] = total[0:2, :]
    gb_ref[oc, 0:2, :] = total[2:4, :]
    stage4(5)

    for cp in p1c:
        cp.wait_send()
    for cp in (g_remote, x_remote, i_copy, halo[0], halo[1]):
        cp.wait_send()
    for qq in range(4):
        z_own(0, qq).wait_send()
        z_own(1, qq).wait_send()
        z_fwd(qq).wait_send()
    for k in range(4):
        for h in range(2):
            cross(k, h).wait_send()
            inner(k, h).wait_send()
    for r in range(1, 8):
        a1_copy(r).wait_send()
    for r in range(1, 16):
        a2_copy(r).wait_send()

    def drain(i, _):
        for k in range(2):
            x_copy(i, k).wait_send()
        for k in range(3):
            z_copy(i, k).wait_send()
        for r in range(1, 8):
            y_copy(i, r).wait_send()
        d_copy(i).wait_send()
        return 0

    lax.fori_loop(0, 6, drain, 0)


def join_halves(ig_ref, fin, gb_ref, out_ref, wg_ref, gg_ref, bg_ref):
    def rows(i, _):
        r = rows16(i * 256, 256)
        both = jnp.concatenate([ig_ref[0, r, :].astype(f32), ig_ref[1, r, :].astype(f32)], axis=1)
        out_ref[r, :] = both.astype(bf16)
        return 0

    lax.fori_loop(0, 4, rows, 0)
    for a in range(3):
        for b in range(3):
            tap = jnp.concatenate([fin[h, a, 0:10, b * HALF : (b + 1) * HALF] for h in range(2)], axis=1)
            wg_ref[:, (3 * a + b) * CH : (3 * a + b + 1) * CH] = tap
    both = jnp.concatenate([gb_ref[0, 0:2, :], gb_ref[1, 0:2, :]], axis=1)
    gg_ref[...] = both[0:1, :].reshape(CH)
    bg_ref[...] = both[1:2, :].reshape(CH)


def on_device(shifted, out_grad, conv_weight, norm_gain, norm_bias, shift_fwd, shift_bwd):
    scale = 131072.0 ** (-0.5)
    x = shifted.reshape(1024, CH)
    g = out_grad.reshape(4, 256, CH)
    dma = pltpu.SemaphoreType.DMA
    vm = pltpu.VMEM
    scratch = [
        vm((2, 240, 128), bf16), vm((1024, CH), bf16),
        vm((2, 1024, HALF), bf16), vm((1024, HALF), bf16), vm((8, 288, CH), bf16), vm((CH, 2048), bf16),
        vm((CH, CH), bf16), vm((8, 288, WIDE), bf16), vm((8, 240, 128), bf16), vm((3, 8, 80, WIDE), bf16),
        vm((2048, WIDE), f32), vm((2048, HALF), f32),
        vm((8, HALF), f32), vm((8, HALF), f32), vm((8, HALF), f32), vm((8, HALF), f32), vm((8, HALF), f32), vm((8, HALF), f32),
        vm((6, HALF, 512), f32), vm((6, 2, HALF, 256), bf16), vm((6, 2, HALF, 256), bf16),
        vm((6, 3, 80, 512), bf16), vm((6, 3, 80, 512), bf16),
        vm((6, 8, 16, 512), f32), vm((6, 8, 16, 512), bf16), vm((6, 8, 16, 512), bf16),
        vm((6, 2, 16, 512), f32), vm((6, 2, 16, 512), f32),
        vm((10, 256, HALF), bf16), vm((4, 256, HALF), bf16), vm((4, 256, HALF), bf16),
        vm((2, 256, 80), bf16), vm((2, 256, 80), bf16), vm((2, HALF, 80), bf16),
        vm((8, HALF), f32), vm((8, 8, HALF), f32), vm((8, HALF), f32), vm((16, 8, HALF), f32),
        dma((2,)), dma((4,)), dma((4,)), dma((7,)), dma((7,)), dma((2, 4)), dma((2, 4)), dma((4,)), dma((4,)),
        dma((4, 2)), dma((4, 2)), dma((4, 2)), dma((4, 2)),
        dma((6, 2)), dma((6, 2)), dma((6, 3)), dma((6, 3)), dma((6, 8)), dma((6, 8)),
        dma((6,)), dma((6,)), dma((2,)), dma((2,)), dma((8,)), dma((8,)), dma((16,)), dma((16,)),
    ]
    v = pl.BlockSpec(memory_space=pltpu.VMEM)

    def body(*refs):
        kernel(scale, *refs)

    parts = pl.pallas_call(
        body,
        out_shape=(
            jax.ShapeDtypeStruct((2, 1024, HALF), bf16),
            jax.ShapeDtypeStruct((2, 3, 16, WIDE), f32),
            jax.ShapeDtypeStruct((2, 8, HALF), f32),
        ),
        in_specs=[pl.BlockSpec(memory_space=pl.ANY), pl.BlockSpec(memory_space=pl.ANY), v, v, v, v, v],
        out_specs=(v, v, v),
        scratch_shapes=scratch,
        compiler_params=pltpu.CompilerParams(collective_id=0, has_side_effects=True, vmem_limit_bytes=60 << 20),
    )(x, g, conv_weight, norm_gain, norm_bias, shift_fwd, shift_bwd)
    ig, wg, gg, bg = pl.pallas_call(
        join_halves,
        out_shape=(
            jax.ShapeDtypeStruct((1024, CH), bf16),
            jax.ShapeDtypeStruct((10, 9 * CH), f32),
            jax.ShapeDtypeStruct((CH,), f32),
            jax.ShapeDtypeStruct((CH,), f32),
        ),
        in_specs=[v, v, v],
        out_specs=(v, v, v, v),
    )(*parts)
    return (ig.reshape(shifted.shape), wg, gg, bg)


def solution(mesh):
    in_specs = (
        P("dp", "frames", None, None, None),
        P("dp", "frames", None, None, None),
        P("frames", None),
        P(),
        P(),
        P(),
        P(),
    )
    out_specs = (P("dp", "frames", None, None, None), P("frames", None), P(), P())
    return jax.shard_map(
        on_device, mesh=mesh, in_specs=in_specs, out_specs=out_specs, check_vma=False
    )
```

```python
import jax
import jax.numpy as jnp
from jax import lax
from jax.experimental import pallas as pl
from jax.experimental.pallas import tpu as pltpu
from jax.sharding import PartitionSpec as P

f32, bf16 = jnp.float32, jnp.bfloat16
MESH = pl.DeviceIdType.MESH
EPS = 1e-05
CH, HALF, WIDE = 640, 320, 1024
HIGH = lax.Precision.HIGHEST


def dot(a, b):
    return jnp.dot(a, b, preferred_element_type=f32)


def dot_nt(a, b):
    return lax.dot_general(a, b, (((1,), (1,)), ((), ())), preferred_element_type=f32)


def rows16(v, n):
    return pl.ds(pl.multiple_of(v, 16), n)


def div20(i):
    return (i * 3277) >> 16


def kernel(
    scale,
    x_hbm, g_hbm, w_ref, gain_ref, bias_ref, fwd_ref, bwd_ref,
    ig_hbm, wg_ref, gg_ref, bg_ref,
    wpc, fin, x_ref, xs, xb, gp, gt, pm, ap, p1, w, y_acc, pre,
    cen, inv, s1, s2, m1, m2,
    s_buf, wgs, xr, z1s, z1r, z2s, z2r, yf, ys, yr, ds_, dr,
    sgp, igs, igr, igo, hs, hr, selm, a1s, a1r, a2s, a2r,
    loc_sem, ex_s, ex_r, p1_s, p1_r, zo_s, zo_r, zf_s, zf_r, cr_s, cr_r, yi_s, yi_r,
    x_s, x_r, z1_ss, z1_rs, z2_ss, z2_rs, y_ss, y_rs, d_ss, d_rs, h_ss, h_rs, a1_ss, a1_rs, a2_ss, a2_rs,
):
    f = lax.axis_index("frames")
    d = lax.axis_index("dp")
    c = f % 2
    xl = (f // 2) % 2
    y = (f // 4) % 4
    z = f // 16
    x = d * 2 + xl
    y0 = y % 2
    y1 = y // 2

    def dev(zz, yy, xx, cc):
        return {"frames": ((zz * 4 + yy) * 2 + xx % 2) * 2 + cc, "dp": xx // 2}

    oc = 1 - c
    zp, zm, zo = (z + 1) % 4, (z + 3) % 4, (z + 2) % 4
    yin = y + 1 - 2 * y0
    ycross = (y + 3 + 2 * y0) % 4
    xin = x + 1 - 2 * xl
    xcross = (x + 3 + 2 * xl) % 4
    xop = (x + 2) % 4
    sib = dev(z, y, x, oc)
    nxt = {"frames": (f + 2) % 64, "dp": d}
    prv = {"frames": (f + 62) % 64, "dp": d}

    def remote(src, dst, ss, rs, to):
        return pltpu.make_async_remote_copy(
            src_ref=src, dst_ref=dst, send_sem=ss, recv_sem=rs, device_id=to, device_id_type=MESH
        )

    barrier = pltpu.get_barrier_semaphore()
    partners = [sib, nxt, prv]
    for yy, xx in ((yin, x), (y, xin), (yin, xin)):
        partners += [dev(z, yy, xx, 0), dev(z, yy, xx, 1)]
    for k in (2, 3):
        yy = (ycross, (y + 2) % 4)[k - 2]
        partners += [dev(z, yy, x, 0), dev(z, yy, x, 1)]
    for xx in (xcross, xop):
        partners += [dev(z, y, xx, 0), dev(z, y, xx, 1)]
    partners += [dev(zz, (y + dy) % 4, x, c) for zz in (zp, zm, zo) for dy in range(4)]
    for to in partners:
        pl.semaphore_signal(barrier, inc=1, device_id=to, device_id_type=MESH)

    x_local = pltpu.make_async_copy(x_hbm, x_ref, loc_sem.at[1])
    x_local.start()
    for h in range(2):
        wide = []
        for a in range(3):
            taps = [w_ref[:, (3 * a + b) * CH + h * HALF : (3 * a + b) * CH + (h + 1) * HALF].astype(f32) for b in range(3)]
            wide.append(jnp.concatenate(taps + [jnp.zeros((10, WIDE - 3 * HALF), f32)], axis=1))
        for half in range(2):
            pieces = [wide[a][:, lb * 128 : lb * 128 + 128] for lb in range(4 * half, 4 * half + 4) for a in range(3)]
            wpc[h, half] = jnp.concatenate(pieces + [jnp.zeros((8, 128), f32)], axis=0).astype(bf16)
    pl.semaphore_wait(barrier, len(partners))
    me8 = (y0 * 2 + xl) * 2 + c
    def p1_all(half):
        seven = p1.at[0:7, half]
        return remote(seven, seven, p1_s.at[half], p1_r.at[half], sib)

    p1c = ([], [])
    for half in range(2):
        k = 0
        for yy, xx, dc in ((yin, xin, 0), (yin, xin, 1), (yin, x, 0), (yin, x, 1), (y, xin, 0), (y, xin, 1), (y, x, 1)):
            cc = c + dc - 2 * c * dc
            to = dev(z, yy, xx, cc)
            p1c[half].append(remote(wpc.at[cc, half], p1.at[me8, half], p1_s.at[half], p1_r.at[half], to))
            k += 1
        for cp in p1c[half]:
            cp.start()
    interior = (pl.ds(c * 4, 4), pl.ds(16, 256))
    g_local = pltpu.make_async_copy(g_hbm, gp.at[interior], loc_sem.at[0])
    g_remote = remote(g_hbm, gp.at[interior], ex_s.at[0], ex_r.at[0], sib)
    g_local.start()
    p1[me8] = wpc[c]

    x_local.wait()
    def split(t, _):
        r = rows16(t * 256, 256)
        v = x_ref[r, :].astype(f32)
        xs[0, r, :] = v[:, :HALF].astype(bf16)
        xs[1, r, :] = v[:, HALF:].astype(bf16)
        return 0

    lax.fori_loop(0, 4, split, 0)
    x_remote = remote(xs.at[oc], xb, ex_s.at[1], ex_r.at[1], sib)
    x_remote.start()
    g_remote.start()

    def read_x(t):
        r = rows16((t % 4) * 256, 256)
        mine = xs[c, r, :]
        other = xb[r, :]
        return jnp.where(t // 4 == c, mine, other).astype(f32)

    zero16 = jnp.zeros((16, CH), bf16)
    zero16w = jnp.zeros((16, WIDE), bf16)
    for t in range(8):
        gp[t, 0:16, :] = zero16
        gp[t, 272:288, :] = zero16
        ap[t, 0:16, :] = zero16w
        ap[t, 272:288, :] = zero16w

    oi = lax.broadcasted_iota(jnp.int32, (CH, CH), 0)
    li = lax.broadcasted_iota(jnp.int32, (CH, CH), 1)
    q = (oi >= HALF).astype(jnp.int32)
    rr = oi - HALF * q
    zy = div20(rr)
    src_row = (2 * zy + (q + xl - 2 * q * xl)) * 20 + (rr - 20 * zy)
    pm[...] = (li == src_row).astype(f32).astype(bf16)
    gi = div20(lax.broadcasted_iota(jnp.int32, (HALF, HALF), 0))
    gj = div20(lax.broadcasted_iota(jnp.int32, (HALF, HALF), 1))
    group_mean = jnp.where(gi == gj, 1.0 / 5120.0, 0.0).astype(f32)

    def spread_groups(v):
        return jnp.dot(v, group_mean, preferred_element_type=f32, precision=HIGH)

    mine0 = c == 0
    gain_all, bias_all = gain_ref[...].reshape(1, CH), bias_ref[...].reshape(1, CH)
    gain = jnp.where(mine0, gain_all[:, :HALF], gain_all[:, HALF:])
    bias = jnp.where(mine0, bias_all[:, :HALF], bias_all[:, HALF:])

    def transpose(t):
        gt[:, pl.ds(pl.multiple_of(t * 256, 256), 256)] = dot_nt(pm[...], gp[t, 16:272, :]).astype(bf16)

    g_local.wait()

    def transpose_mine(i, _):
        transpose(c * 4 + i)
        return 0

    lax.fori_loop(0, 4, transpose_mine, 0)

    blk = z * 2 + y1

    def dense(half):
        p1_all(half).wait_recv()
        for lb in range(4):
            for a in range(3):
                r = (lb * 3 + a) * 10
                piece = jnp.concatenate([p1[s, half, r : r + 10, :].astype(f32) for s in range(8)], axis=0)
                at = (half * 4 + lb) * 128
                w[a, blk, :, at : at + 128] = piece.astype(bf16)

    dense(0)

    def lanes(qq, n=256):
        return pl.ds(pl.multiple_of(qq * 256, 256), n)

    def wsl(b, qq):
        return w.at[:, b, :, lanes(qq)]

    def quarter(j):
        return (2 * (j % 2) + 1 - y0) if j < 2 else (2 * (j % 2) + y0)

    def z_own(k, j):
        s = wsl(blk, quarter(j))
        return remote(s, s, zo_s.at[0], zo_r.at[j], dev((zp, zm)[k], y, x, c))

    def z_fwd(j):
        up = j % 2 == 0
        s = wsl((zm if up else zp) * 2 + y1, quarter(j))
        return remote(s, s, zf_s.at[0], zf_r.at[j], dev(zp if up else zm, y, x, c))

    zrel = (z, zm, zp, zo)

    def cross(k, h):
        s = wsl(zrel[k] * 2 + y1, 2 * h + 1 - y0)
        return remote(s, s, cr_s.at[0], cr_r.at[k, h], dev(z, ycross, x, c))

    def inner(k, h):
        s = wsl(zrel[k] * 2 + 1 - y1, 2 * h + y0)
        return remote(s, s, yi_s.at[0], yi_r.at[h], dev(z, yin, x, c))

    def inner_all(h):
        one = w.at[:, 0]
        return remote(one, one, yi_s.at[0], yi_r.at[h], sib)

    def z_start(j):
        z_own(0, j).start()
        z_own(1, j).start()

    def z_wait(j):
        two = w.at[:, 0:2, :, 0:256]
        remote(two, two, zo_s.at[0], zo_r.at[j], sib).wait_recv()

    def hook_in(k, h):
        cross(k, h).wait_recv()
        inner(k, h).start()

    def hook0():
        dense(1)
        z_start(1)
        cross(0, 1).start()

    def hook1():
        z_wait(0)
        z_fwd(0).start()
        cross(1, 0).start()
        hook_in(0, 0)
        z_start(2)

    def hook2():
        cross(2, 0).start()

    def hook3():
        z_wait(1)
        z_fwd(1).start()
        hook_in(0, 1)
        z_start(3)

    def hook4():
        z_fwd(0).wait_recv()
        cross(3, 0).start()
        hook_in(1, 0)

    def hook5():
        cross(1, 1).start()
        z_wait(2)
        z_fwd(2).start()

    def hook6():
        hook_in(2, 0)
        z_fwd(1).wait_recv()
        cross(2, 1).start()

    def hook7():
        hook_in(3, 0)
        cross(3, 1).start()

    def hook8():
        hook_in(1, 1)
        z_wait(3)
        z_fwd(3).start()

    cross(0, 0).start()
    z_start(0)

    x_remote.wait_recv()

    def stat_sum(t, _):
        s1[pl.ds(t, 1), :] = jnp.sum(read_x(t), axis=0, keepdims=True)
        return 0

    lax.fori_loop(0, 8, stat_sum, 0)
    cen[...] = spread_groups(s1[...])

    def stat_sq(t, _):
        v = read_x(t) - cen[pl.ds(t, 1), :]
        s2[pl.ds(t, 1), :] = jnp.sum(v * v, axis=0, keepdims=True)
        return 0

    lax.fori_loop(0, 8, stat_sq, 0)
    inv[...] = lax.rsqrt(spread_groups(s2[...]) + EPS)

    hook0()
    col = lax.broadcasted_iota(jnp.int32, (256, HALF), 0) % 16

    def normed_of(t):
        return (read_x(t) - cen[pl.ds(t, 1), :]) * inv[pl.ds(t, 1), :]

    def forward(t, _):
        before = normed_of(t) * gain + bias
        act = before / (1.0 + jnp.exp(-before))
        left = jnp.where(col == 0, 0.0, pltpu.roll(act, 1, 0))
        right = jnp.where(col == 15, 0.0, pltpu.roll(act, 255, 0))
        cat = jnp.concatenate([left, act, right, jnp.zeros((256, WIDE - 3 * HALF), f32)], axis=1)
        ap[t, 16:272, :] = cat.astype(bf16)
        return 0

    g_remote.wait_recv()

    def forward_pair(i, _):
        transpose(oc * 4 + i)
        forward(2 * i, 0)
        forward(2 * i + 1, 0)
        pl.when(i == 1)(hook1)
        return 0

    lax.fori_loop(0, 4, forward_pair, 0)
    hook2()

    def x_copy(i, k):
        to = (xin, xcross)[k]
        return remote(wgs.at[i, k], xr.at[i, k], x_s.at[0], x_r.at[i], dev(z, y, to, c))

    def x_all(i):
        return remote(wgs.at[i], xr.at[i], x_s.at[0], x_r.at[i], sib)

    def wg_step(i, _):
        a, n = i // 2, i % 2
        cols = pl.ds(pl.multiple_of(n * 512, 512), 512)
        acc = None
        for t in range(8):
            v = dot(gt[:, t * 256 : t * 256 + 256], ap[t, rows16(a * 16, 256), cols])
            acc = v if acc is None else acc + v
        s_buf[i] = acc[:HALF, :]
        wgs[i, 0] = acc[HALF:, :256].astype(bf16)
        wgs[i, 1] = acc[HALF:, 256:].astype(bf16)
        x_copy(i, 0).start()
        x_copy(i, 1).start()

        for k, hook in enumerate((hook3, hook4, hook5, hook6, hook7, hook8)):
            pl.when(i == k)(hook)
        pl.when(i == 4)(lambda: stage1(0))
        return 0

    def z1_copy(i, k):
        return remote(z1s.at[i, k], z1r.at[i, k], z1_ss.at[0], z1_rs.at[i], dev((zp, zm)[k], y, x, c))

    def z1_all(i):
        return remote(z1s.at[i], z1r.at[i], z1_ss.at[0], z1_rs.at[i], sib)

    def z2_copy(i, k):
        return remote(z2s.at[i, k], z2r.at[i, k], z2_ss.at[0], z2_rs.at[i], dev((zp, zm)[k], y, x, c))

    def z2_all(i):
        return remote(z2s.at[i], z2r.at[i], z2_ss.at[0], z2_rs.at[i], sib)

    def y_copy(i, r):
        dy, dc = r // 2, r % 2
        yy, cc = (y + dy) % 4, c + dc - 2 * c * dc
        return remote(ys.at[i, yy * 2 + cc], yr.at[i, r], y_ss.at[0], y_rs.at[i], dev(z, yy, x, cc))

    def y_all(i):
        seven = yr.at[i, 1:8]
        return remote(seven, seven, y_ss.at[0], y_rs.at[i], sib)

    def d_copy(i):
        return remote(ds_.at[i], dr.at[i], d_ss.at[0], d_rs.at[0], dev(z, y, xop, c))

    def block(b):
        return rows16(b * 80, 80)

    def stage1(i):
        x_all(i).wait_recv()
        s_buf[i, :, :256] = s_buf[i, :, :256] + xr[i, 0].astype(f32)
        s_buf[i, :, 256:] = s_buf[i, :, 256:] + xr[i, 1].astype(f32)
        z1s[i, 0] = s_buf[i, block(zo), 0:256].astype(bf16)
        z1s[i, 1] = s_buf[i, block(zo), 256:512].astype(bf16)
        z1_copy(i, 0).start()
        z1_copy(i, 1).start()

    def relay(i):
        z1_all(i).wait_recv()
        z2s[i, 0, :, 0:256] = (s_buf[i, block(zp), 0:256] + z1r[i, 0].astype(f32)).astype(bf16)
        z2s[i, 0, :, 256:512] = s_buf[i, block(zp), 256:512].astype(bf16)
        z2_copy(i, 0).start()
        z2s[i, 1, :, 0:256] = s_buf[i, block(zm), 0:256].astype(bf16)
        z2s[i, 1, :, 256:512] = (s_buf[i, block(zm), 256:512] + z1r[i, 1].astype(f32)).astype(bf16)
        z2_copy(i, 1).start()

    def stage2(i):
        z2_all(i).wait_recv()
        total = s_buf[i, block(z), :] + z2r[i, 0].astype(f32) + z2r[i, 1].astype(f32)
        total = jnp.concatenate([total, jnp.zeros((8, 512), f32)], axis=0)
        for k in range(8):
            piece = total[10 * k : 10 * k + 16, :]
            yf[i, k] = piece
            ys[i, k] = piece.astype(bf16)
        for r in range(1, 8):
            y_copy(i, r).start()

    def stage3(i):
        y_all(i).wait_recv()
        own = yf[i, y * 2 + c]
        for dy in (1, 2, 3):
            own = own + yr[i, 2 * dy].astype(f32)
        other = yr[i, 1].astype(f32)
        for dy in (1, 2, 3):
            other = other + yr[i, 2 * dy + 1].astype(f32)
        ds_[i, 0] = own
        ds_[i, 1] = other
        d_copy(i).start()

    def stage4(i):
        own = (ds_[i, 0] + dr[i, 0]) * scale
        other = (ds_[i, 1] + dr[i, 1]) * scale
        a, n = i // 2, i % 2
        cols = pl.ds(pl.multiple_of(n * 512, 512), 512)
        fin[0, a, :, cols] = jnp.where(mine0, own, other)
        fin[1, a, :, cols] = jnp.where(mine0, other, own)

    lax.fori_loop(0, 6, wg_step, 0)
    stage1(1)
    relay(0)
    inner_all(0).wait_recv()
    z_fwd(2).wait_recv()

    def back1(t, _):
        r = rows16(t * 256, 256)
        v = y_acc[r, :]
        right = jnp.where(col == 15, 0.0, pltpu.roll(v[:, :HALF], 255, 0))
        left = jnp.where(col == 0, 0.0, pltpu.roll(v[:, 2 * HALF : 3 * HALF], 1, 0))
        act_grad = right + v[:, HALF : 2 * HALF] + left
        normed = normed_of(t)
        before = normed * gain + bias
        g = 1.0 / (1.0 + jnp.exp(-before))
        p = act_grad * g * (1.0 + before * (1.0 - g))
        pre[r, :] = p
        s1[pl.ds(t, 1), :] = jnp.sum(p * normed, axis=0, keepdims=True)
        s2[pl.ds(t, 1), :] = jnp.sum(p, axis=0, keepdims=True)
        return 0

    def back2(t, _):
        r = rows16(t * 256, 256)
        v = pre[r, :] * gain - m1[pl.ds(t, 1), :] - normed_of(t) * m2[pl.ds(t, 1), :]
        sgp[t + 1] = (v * inv[pl.ds(t, 1), :]).astype(bf16)
        return 0

    def back1_of(frames):
        for t in frames:
            back1(t, 0)

    def group_terms():
        both = spread_groups(jnp.concatenate([s2[...] * gain, s1[...] * gain], axis=0))
        m1[...] = both[0:8]
        m2[...] = both[8:16]

    halo = [
        remote(hs.at[0], hr.at[0], h_ss.at[0], h_rs.at[0], nxt),
        remote(hs.at[1], hr.at[1], h_ss.at[1], h_rs.at[1], prv),
    ]
    ch_id = lax.broadcasted_iota(jnp.int32, (HALF, 80), 0) + c * HALF
    selm[0] = (ch_id == bwd_ref[...].reshape(1, 80)).astype(f32).astype(bf16)
    selm[1] = (ch_id == fwd_ref[...].reshape(1, 80)).astype(f32).astype(bf16)

    def edge_frames():
        group_terms()
        back2(0, 0)
        back2(7, 0)
        hs[0] = dot(sgp[8], selm[0]).astype(bf16)
        hs[1] = dot(sgp[1], selm[1]).astype(bf16)
        halo[0].start()
        halo[1].start()

    def act_dot(n, tt):
        cols = pl.ds(n * 512, 512)
        lhs = jnp.concatenate(
            [
                jnp.concatenate([gp[tt * 2 + t, 16 * (2 - a) : 16 * (2 - a) + 256, :] for a in range(3)], axis=1)
                for t in range(2)
            ],
            axis=0,
        )
        rhs = w[:, :, :, cols].reshape(3 * CH, 512)
        y_acc[rows16(tt * 512, 512), cols] = dot(lhs, rhs)

    def act_step(i, _):
        act_dot(0, i)
        plan = {
            0: [(stage1, 2), (relay, 1)],
            1: [(stage2, 0)],
            2: [(stage1, 3)],
            3: [(relay, 2), (stage2, 1)],
        }
        for k in range(4):

            @pl.when(i == k)
            def _(k=k):
                if k == 0:
                    hook_in(2, 1)
                if k == 2:
                    hook_in(3, 1)
                for stage, chunk in plan.get(k, []):
                    stage(chunk)

        return 0

    lax.fori_loop(0, 4, act_step, 0)
    stage1(4)
    inner_all(1).wait_recv()
    z_fwd(3).wait_recv()
    act_dot(1, 3)
    relay(3)
    act_dot(1, 0)
    back1_of((6, 7))
    stage1(5)
    relay(4)
    stage2(2)
    act_dot(1, 1)
    back1_of((0, 1))
    stage3(0)
    edge_frames()
    act_dot(1, 2)
    stage2(3)
    relay(5)
    back1_of((2, 3))
    stage3(1)

    def a1_copy(r):
        dx, dc = r // 2, r % 2
        cc = c + dc - 2 * c * dc
        return remote(a1s, a1r.at[r], a1_ss.at[0], a1_rs.at[0], dev(z, y, (x + dx) % 4, cc))

    def a2_copy(r):
        return remote(a2s, a2r.at[r], a2_ss.at[0], a2_rs.at[0], dev((z + r // 4) % 4, (y + r % 4) % 4, x, c))

    a1_all = remote(a1r.at[1:8], a1r.at[1:8], a1_ss.at[0], a1_rs.at[0], sib)
    a2_all = remote(a2r.at[1:16], a2r.at[1:16], a2_ss.at[0], a2_rs.at[0], sib)

    back1_of((4, 5))
    total = [jnp.sum(v[...], axis=0, keepdims=True) for v in (s1, s2)]
    a1s[...] = jnp.concatenate(total + [jnp.zeros((6, HALF), f32)], axis=0)
    for r in range(1, 8):
        a1_copy(r).start()
    stage2(4)
    group_terms()
    lax.fori_loop(1, 7, back2, 0)
    stage3(2)
    stage2(5)
    halo[0].wait_recv()
    halo[1].wait_recv()
    keep_prev = jnp.where(f >= 2, 1.0, 0.0)
    keep_next = jnp.where(f < 62, 1.0, 0.0)
    sgp[0] = (dot_nt(hr[0], selm[0]) * keep_prev).astype(bf16)
    sgp[9] = (dot_nt(hr[1], selm[1]) * keep_next).astype(bf16)
    ones = jnp.ones((8, 80), bf16)
    bwd_mask = dot_nt(ones, selm[0])[0:1, :] > 0.5
    fwd_mask = dot_nt(ones, selm[1])[0:1, :] > 0.5

    def shift(t):
        v = jnp.where(bwd_mask, sgp[t].astype(f32), sgp[t + 1].astype(f32))
        return jnp.where(fwd_mask, sgp[t + 2].astype(f32), v)

    def shift_other(i, _):
        igs[i] = shift(oc * 4 + i).astype(bf16)
        return 0

    lax.fori_loop(0, 4, shift_other, 0)
    i_copy = remote(igs, igr, ex_s.at[2], ex_r.at[2], sib)
    i_copy.start()
    a1_all.wait_recv()
    own = a1s[0:2, :]
    for r in (2, 4, 6):
        own = own + a1r[r, 0:2, :]
    other = a1r[1, 0:2, :]
    for r in (3, 5, 7):
        other = other + a1r[r, 0:2, :]
    a2s[...] = jnp.concatenate([own, other, jnp.zeros((4, HALF), f32)], axis=0)
    for r in range(1, 16):
        a2_copy(r).start()
    stage3(3)
    stage3(4)
    stage3(5)
    i_copy.wait_recv()

    def assemble(i, _):
        own = shift(c * 4 + i)
        other = igr[i].astype(f32)
        v = jnp.concatenate([jnp.where(mine0, own, other), jnp.where(mine0, other, own)], axis=1)
        igo[rows16(i * 256, 256), :] = v.astype(bf16)
        return 0

    lax.fori_loop(0, 4, assemble, 0)
    o_copy = pltpu.make_async_copy(igo, ig_hbm, loc_sem.at[2])
    o_copy.start()

    p1_all(0).wait_send()
    p1_all(1).wait_send()
    for cp in (g_remote, x_remote, i_copy, halo[0], halo[1]):
        cp.wait_send()
    one, two = w.at[:, 0], w.at[:, 0:2]
    for ref, sem in ((two, zo_s), (one, zf_s), (two, cr_s), (two, yi_s), (wgs, x_s), (z1s, z1_ss), (z2s, z2_ss), (yr.at[:, 1:8], y_ss)):
        remote(ref, ref, sem.at[0], sem.at[0], sib).wait_send()
    a1_all.wait_send()

    remote(ds_, dr, d_ss.at[0], d_rs.at[0], sib).wait_recv()
    for i in range(6):
        stage4(i)
    for a in range(3):
        for b in range(3):
            tap = jnp.concatenate([fin[h, a, 0:10, b * HALF : (b + 1) * HALF] for h in range(2)], axis=1)
            wg_ref[:, (3 * a + b) * CH : (3 * a + b + 1) * CH] = tap
    total = a2s[...]
    a2_all.wait_recv()
    for r in range(1, 16):
        total = total + a2r[r]
    total = total * scale
    own, other = total[0:2, :], total[2:4, :]
    both = jnp.concatenate([jnp.where(mine0, own, other), jnp.where(mine0, other, own)], axis=1)
    gg_ref[...] = both[0:1, :].reshape(CH)
    bg_ref[...] = both[1:2, :].reshape(CH)
    a2_all.wait_send()
    remote(ds_, dr, d_ss.at[0], d_rs.at[0], sib).wait_send()
    o_copy.wait()


def hand_over(ig_in, wg_in, gg_in, bg_in, ig_out, wg_out, gg_out, bg_out, ig, wg, gg, bg, in_sem, out_sem):
    rows = [pl.ds(256 * k, 256) for k in range(4)]
    sets = [(ig_in.at[r], ig.at[r], ig_out.at[r]) for r in rows]
    sets += [(wg_in, wg, wg_out), (gg_in, gg, gg_out), (bg_in, bg, bg_out)]
    first = [pltpu.make_async_copy(a, b, in_sem.at[k]) for k, (a, b, _) in enumerate(sets)]
    second = [pltpu.make_async_copy(b, d, out_sem.at[k]) for k, (_, b, d) in enumerate(sets)]
    for cp in first:
        cp.start()
    for a, b in zip(first, second):
        a.wait()
        b.start()
    for cp in second:
        cp.wait()


def on_device(shifted, out_grad, conv_weight, norm_gain, norm_bias, shift_fwd, shift_bwd):
    scale = 131072.0 ** (-0.5)
    x = shifted.reshape(1024, CH)
    g = out_grad.reshape(4, 256, CH)
    dma = pltpu.SemaphoreType.DMA
    vm = pltpu.VMEM
    scratch = [
        vm((2, 2, 128, 128), bf16), vm((2, 3, 16, WIDE), f32), vm((1024, CH), bf16),
        vm((2, 1024, HALF), bf16), vm((1024, HALF), bf16), vm((8, 288, CH), bf16), vm((CH, 2048), bf16),
        vm((CH, CH), bf16), vm((8, 288, WIDE), bf16), vm((8, 2, 128, 128), bf16), vm((3, 8, 80, WIDE), bf16),
        vm((2048, WIDE), f32), vm((2048, HALF), f32),
        vm((8, HALF), f32), vm((8, HALF), f32), vm((8, HALF), f32), vm((8, HALF), f32), vm((8, HALF), f32), vm((8, HALF), f32),
        vm((6, HALF, 512), f32), vm((6, 2, HALF, 256), bf16), vm((6, 2, HALF, 256), bf16),
        vm((6, 2, 80, 256), bf16), vm((6, 2, 80, 256), bf16), vm((6, 2, 80, 512), bf16), vm((6, 2, 80, 512), bf16),
        vm((6, 8, 16, 512), f32), vm((6, 8, 16, 512), bf16), vm((6, 8, 16, 512), bf16),
        vm((6, 2, 16, 512), f32), vm((6, 2, 16, 512), f32),
        vm((10, 256, HALF), bf16), vm((4, 256, HALF), bf16), vm((4, 256, HALF), bf16), vm((1024, CH), bf16),
        vm((2, 256, 80), bf16), vm((2, 256, 80), bf16), vm((2, HALF, 80), bf16),
        vm((8, HALF), f32), vm((8, 8, HALF), f32), vm((8, HALF), f32), vm((16, 8, HALF), f32),
        dma((4,)), dma((4,)), dma((4,)), dma((2,)), dma((2,)), dma((1,)), dma((4,)), dma((1,)), dma((4,)),
        dma((1,)), dma((4, 2)), dma((1,)), dma((2,)),
        dma((1,)), dma((6,)), dma((1,)), dma((6,)), dma((1,)), dma((6,)), dma((1,)), dma((6,)),
        dma((1,)), dma((1,)), dma((2,)), dma((2,)), dma((1,)), dma((1,)), dma((1,)), dma((1,)),
    ]
    v = pl.BlockSpec(memory_space=pltpu.VMEM)

    def body(*refs):
        kernel(scale, *refs)

    shapes = (
        jax.ShapeDtypeStruct((1024, CH), bf16),
        jax.ShapeDtypeStruct((10, 9 * CH), f32),
        jax.ShapeDtypeStruct((CH,), f32),
        jax.ShapeDtypeStruct((CH,), f32),
    )
    anywhere = pl.BlockSpec(memory_space=pl.ANY)
    parts = pl.pallas_call(
        body,
        out_shape=shapes,
        in_specs=[pl.BlockSpec(memory_space=pl.ANY), pl.BlockSpec(memory_space=pl.ANY), v, v, v, v, v],
        out_specs=(anywhere, v, v, v),
        scratch_shapes=scratch,
        compiler_params=pltpu.CompilerParams(collective_id=0, has_side_effects=True, vmem_limit_bytes=60 << 20),
    )(x, g, conv_weight, norm_gain, norm_bias, shift_fwd, shift_bwd)
    ig, wg, gg, bg = pl.pallas_call(
        hand_over,
        out_shape=shapes,
        in_specs=[anywhere] * 4,
        out_specs=(anywhere,) * 4,
        scratch_shapes=[
            vm((1024, CH), bf16), vm((10, 9 * CH), f32), vm((CH,), f32), vm((CH,), f32), dma((7,)), dma((7,)),
        ],
    )(*parts)
    return (ig.reshape(shifted.shape), wg, gg, bg)


def solution(mesh):
    in_specs = (
        P("dp", "frames", None, None, None),
        P("dp", "frames", None, None, None),
        P("frames", None),
        P(),
        P(),
        P(),
        P(),
    )
    out_specs = (P("dp", "frames", None, None, None), P("frames", None), P(), P())
    return jax.shard_map(
        on_device, mesh=mesh, in_specs=in_specs, out_specs=out_specs, check_vma=False
    )
```

```python
import jax
import jax.numpy as jnp
from jax import lax
from jax.experimental import pallas as pl
from jax.experimental.pallas import tpu as pltpu
from jax.sharding import PartitionSpec as P

f32, bf16 = jnp.float32, jnp.bfloat16
MESH = pl.DeviceIdType.MESH
EPS = 1e-05
CH, HALF, WIDE = 640, 320, 1024
FULL = 384
HIGH = lax.Precision.HIGHEST


def dot(a, b):
    return jnp.dot(a, b, preferred_element_type=f32)


def dot_nt(a, b):
    return lax.dot_general(a, b, (((1,), (1,)), ((), ())), preferred_element_type=f32)


def rows16(v, n):
    return pl.ds(pl.multiple_of(v, 16), n)


def div20(i):
    return (i * 3277) >> 16


def kernel(
    scale,
    x_hbm, g_hbm, w_ref, gain_ref, bias_ref, fwd_ref, bwd_ref,
    ig_hbm, wg_ref, gg_ref, bg_ref,
    wpc, fin, x_ref, xs, xb, gp, gt, pm, ap, p1, w, y_acc, pre,
    cen, inv, s1, s2, m1, m2,
    s_buf, wgs, xr, z1s, z1r, z2s, z2r, yf, ys, yr, ds_, dr,
    sgp, igs, igr, igo, hs, hr, selm, a1s, a1r, a2s, a2r,
    loc_sem, ex_s, ex_r, p1_s, p1_r, zo_s, zo_r, zf_s, zf_r, cr_s, cr_r, yi_s, yi_r,
    x_s, x_r, z1_ss, z1_rs, z2_ss, z2_rs, y_ss, y_rs, d_ss, d_rs, h_ss, h_rs, a1_ss, a1_rs, a2_ss, a2_rs,
):
    f = lax.axis_index("frames")
    d = lax.axis_index("dp")
    c = f % 2
    xl = (f // 2) % 2
    y = (f // 4) % 4
    z = f // 16
    x = d * 2 + xl
    y0 = y % 2
    y1 = y // 2

    def dev(zz, yy, xx, cc):
        return {"frames": ((zz * 4 + yy) * 2 + xx % 2) * 2 + cc, "dp": xx // 2}

    oc = 1 - c
    zp, zm, zo = (z + 1) % 4, (z + 3) % 4, (z + 2) % 4
    yin = y + 1 - 2 * y0
    ycross = (y + 3 + 2 * y0) % 4
    xin = x + 1 - 2 * xl
    xcross = (x + 3 + 2 * xl) % 4
    xop = (x + 2) % 4
    sib = dev(z, y, x, oc)
    nxt = {"frames": (f + 2) % 64, "dp": d}
    prv = {"frames": (f + 62) % 64, "dp": d}

    def remote(src, dst, ss, rs, to):
        return pltpu.make_async_remote_copy(
            src_ref=src, dst_ref=dst, send_sem=ss, recv_sem=rs, device_id=to, device_id_type=MESH
        )

    barrier = pltpu.get_barrier_semaphore()
    partners = [sib, nxt, prv]
    for yy, xx in ((yin, x), (y, xin), (yin, xin)):
        partners += [dev(z, yy, xx, 0), dev(z, yy, xx, 1)]
    for k in (2, 3):
        yy = (ycross, (y + 2) % 4)[k - 2]
        partners += [dev(z, yy, x, 0), dev(z, yy, x, 1)]
    for xx in (xcross, xop):
        partners += [dev(z, y, xx, 0), dev(z, y, xx, 1)]
    partners += [dev(zz, (y + dy) % 4, x, c) for zz in (zp, zm, zo) for dy in range(4)]
    for to in partners:
        pl.semaphore_signal(barrier, inc=1, device_id=to, device_id_type=MESH)

    x_local = pltpu.make_async_copy(x_hbm, x_ref, loc_sem.at[1])
    x_local.start()
    for h in range(2):
        wide = []
        for a in range(3):
            taps = [w_ref[:, (3 * a + b) * CH + h * HALF : (3 * a + b) * CH + (h + 1) * HALF].astype(f32) for b in range(3)]
            wide.append(jnp.concatenate(taps + [jnp.zeros((10, WIDE - 3 * HALF), f32)], axis=1))
        for half in range(2):
            pieces = [wide[a][:, lb * 128 : lb * 128 + 128] for lb in range(4 * half, 4 * half + 4) for a in range(3)]
            wpc[h, half] = jnp.concatenate(pieces + [jnp.zeros((8, 128), f32)], axis=0).astype(bf16)
    pl.semaphore_wait(barrier, len(partners))
    me8 = (y0 * 2 + xl) * 2 + c
    def p1_all(half):
        seven = p1.at[0:7, half]
        return remote(seven, seven, p1_s.at[half], p1_r.at[half], sib)

    p1c = ([], [])
    for half in range(2):
        k = 0
        for yy, xx, dc in ((yin, xin, 0), (yin, xin, 1), (yin, x, 0), (yin, x, 1), (y, xin, 0), (y, xin, 1), (y, x, 1)):
            cc = c + dc - 2 * c * dc
            to = dev(z, yy, xx, cc)
            p1c[half].append(remote(wpc.at[cc, half], p1.at[me8, half], p1_s.at[half], p1_r.at[half], to))
            k += 1
    for cp in p1c[0]:
        cp.start()
    interior = (pl.ds(c * 4, 4), pl.ds(16, 256))
    g_local = pltpu.make_async_copy(g_hbm, gp.at[interior], loc_sem.at[0])
    g_remote = remote(g_hbm, gp.at[interior], ex_s.at[0], ex_r.at[0], sib)
    g_local.start()
    p1[me8] = wpc[c]

    x_local.wait()
    def split(t, _):
        r = rows16(t * 256, 256)
        v = x_ref[r, :].astype(f32)
        xs[0, r, :HALF] = v[:, :HALF].astype(bf16)
        xs[1, r, :HALF] = v[:, HALF:].astype(bf16)
        return 0

    lax.fori_loop(0, 4, split, 0)
    x_remote = remote(xs.at[oc], xb, ex_s.at[1], ex_r.at[1], sib)
    x_remote.start()
    g_remote.start()

    def read_x(t):
        r = rows16((t % 4) * 256, 256)
        mine = xs[c, r, :HALF]
        other = xb[r, :HALF]
        return jnp.where(t // 4 == c, mine, other).astype(f32)

    zero16 = jnp.zeros((16, CH), bf16)
    zero16w = jnp.zeros((16, WIDE), bf16)
    for t in range(8):
        gp[t, 0:16, :] = zero16
        gp[t, 272:288, :] = zero16
        ap[t, 0:16, :] = zero16w
        ap[t, 272:288, :] = zero16w

    oi = lax.broadcasted_iota(jnp.int32, (CH, CH), 0)
    li = lax.broadcasted_iota(jnp.int32, (CH, CH), 1)
    q = (oi >= HALF).astype(jnp.int32)
    rr = oi - HALF * q
    zy = div20(rr)
    src_row = (2 * zy + (q + xl - 2 * q * xl)) * 20 + (rr - 20 * zy)
    pm[...] = (li == src_row).astype(f32).astype(bf16)
    gi = div20(lax.broadcasted_iota(jnp.int32, (HALF, HALF), 0))
    gj = div20(lax.broadcasted_iota(jnp.int32, (HALF, HALF), 1))
    group_mean = jnp.where(gi == gj, 1.0 / 5120.0, 0.0).astype(f32)

    def spread_groups(v):
        return jnp.dot(v, group_mean, preferred_element_type=f32, precision=HIGH)

    mine0 = c == 0
    gain_all, bias_all = gain_ref[...].reshape(1, CH), bias_ref[...].reshape(1, CH)
    gain = jnp.where(mine0, gain_all[:, :HALF], gain_all[:, HALF:])
    bias = jnp.where(mine0, bias_all[:, :HALF], bias_all[:, HALF:])

    def transpose(t):
        gt[:, pl.ds(pl.multiple_of(t * 256, 256), 256)] = dot_nt(pm[...], gp[t, 16:272, :]).astype(bf16)

    g_local.wait()

    def transpose_mine(i, _):
        transpose(c * 4 + i)
        return 0

    lax.fori_loop(0, 4, transpose_mine, 0)
    for cp in p1c[1]:
        cp.start()

    x_remote.wait_recv()

    def stat_sum(t, _):
        s1[pl.ds(t, 1), :] = jnp.sum(read_x(t), axis=0, keepdims=True)
        return 0

    lax.fori_loop(0, 8, stat_sum, 0)
    cen[...] = spread_groups(s1[...])

    def stat_sq(t, _):
        v = read_x(t) - cen[pl.ds(t, 1), :]
        s2[pl.ds(t, 1), :] = jnp.sum(v * v, axis=0, keepdims=True)
        return 0

    lax.fori_loop(0, 8, stat_sq, 0)
    inv[...] = lax.rsqrt(spread_groups(s2[...]) + EPS)

    blk = z * 2 + y1

    def dense(half):
        p1_all(half).wait_recv()
        for lb in range(4):
            for a in range(3):
                r = (lb * 3 + a) * 10
                piece = jnp.concatenate([p1[s, half, r : r + 10, :].astype(f32) for s in range(8)], axis=0)
                at = (half * 4 + lb) * 128
                w[a, blk, :, at : at + 128] = piece.astype(bf16)

    dense(0)

    def lanes(qq, n=256):
        return pl.ds(pl.multiple_of(qq * 256, 256), n)

    def wsl(b, qq):
        return w.at[:, b, :, lanes(qq)]

    def quarter(j):
        return (2 * (j % 2) + 1 - y0) if j < 2 else (2 * (j % 2) + y0)

    def z_own(k, j):
        s = wsl(blk, quarter(j))
        return remote(s, s, zo_s.at[0], zo_r.at[j], dev((zp, zm)[k], y, x, c))

    def z_fwd(j):
        up = j % 2 == 0
        s = wsl((zm if up else zp) * 2 + y1, quarter(j))
        return remote(s, s, zf_s.at[0], zf_r.at[j], dev(zp if up else zm, y, x, c))

    zrel = (z, zm, zp, zo)

    def cross(k, h):
        s = wsl(zrel[k] * 2 + y1, 2 * h + 1 - y0)
        return remote(s, s, cr_s.at[0], cr_r.at[k, h], dev(z, ycross, x, c))

    def inner(k, h):
        s = wsl(zrel[k] * 2 + 1 - y1, 2 * h + y0)
        return remote(s, s, yi_s.at[0], yi_r.at[h], dev(z, yin, x, c))

    def inner_all(h):
        one = w.at[:, 0]
        return remote(one, one, yi_s.at[0], yi_r.at[h], sib)

    def z_start(j):
        z_own(0, j).start()
        z_own(1, j).start()

    def z_wait(j):
        two = w.at[:, 0:2, :, 0:256]
        remote(two, two, zo_s.at[0], zo_r.at[j], sib).wait_recv()

    def hook_in(k, h):
        cross(k, h).wait_recv()
        inner(k, h).start()

    def hook0():
        dense(1)
        z_start(1)
        cross(0, 1).start()

    def hook1():
        z_wait(0)
        z_fwd(0).start()
        cross(1, 0).start()
        hook_in(0, 0)
        z_start(2)

    def hook2():
        cross(2, 0).start()

    def hook3():
        z_wait(1)
        z_fwd(1).start()
        hook_in(0, 1)
        z_start(3)

    def hook4():
        z_fwd(0).wait_recv()
        cross(3, 0).start()
        hook_in(1, 0)

    def hook5():
        cross(1, 1).start()
        z_wait(2)
        z_fwd(2).start()

    def hook6():
        hook_in(2, 0)
        z_fwd(1).wait_recv()
        cross(2, 1).start()

    def hook7():
        hook_in(3, 0)
        cross(3, 1).start()

    def hook8():
        hook_in(1, 1)
        z_wait(3)
        z_fwd(3).start()

    cross(0, 0).start()
    z_start(0)

    col = lax.broadcasted_iota(jnp.int32, (256, HALF), 0) % 16

    def normed_of(t):
        return (read_x(t) - cen[pl.ds(t, 1), :]) * inv[pl.ds(t, 1), :]

    def forward(t, _):
        before = normed_of(t) * gain + bias
        act = before / (1.0 + jnp.exp(-before))
        left = jnp.where(col == 0, 0.0, pltpu.roll(act, 1, 0))
        right = jnp.where(col == 15, 0.0, pltpu.roll(act, 255, 0))
        cat = jnp.concatenate([left, act, right, jnp.zeros((256, WIDE - 3 * HALF), f32)], axis=1)
        ap[t, 16:272, :] = cat.astype(bf16)
        return 0

    g_remote.wait_recv()

    def forward_pair(i, _):
        transpose(oc * 4 + i)
        forward(2 * i, 0)
        forward(2 * i + 1, 0)
        pl.when(i == 1)(hook0)
        return 0

    lax.fori_loop(0, 4, forward_pair, 0)
    hook1()

    def x_copy(i, k):
        to = (xin, xcross)[k]
        return remote(wgs.at[i, k], xr.at[i, k], x_s.at[0], x_r.at[i], dev(z, y, to, c))

    def x_all(i):
        return remote(wgs.at[i], xr.at[i], x_s.at[0], x_r.at[i], sib)

    def wg_step(i, _):
        a, n = i // 2, i % 2
        cols = pl.ds(pl.multiple_of(n * 512, 512), 512)
        acc = None
        for t in range(8):
            v = dot(gt[:, t * 256 : t * 256 + 256], ap[t, rows16(a * 16, 256), cols])
            acc = v if acc is None else acc + v
        s_buf[i] = acc[:HALF, :]
        wgs[i, 0] = acc[HALF:, :256].astype(bf16)
        wgs[i, 1] = acc[HALF:, 256:].astype(bf16)
        x_copy(i, 0).start()
        x_copy(i, 1).start()

        for k, hook in enumerate((hook2, hook3, hook4, hook5, hook6, hook7)):
            pl.when(i == k)(hook)
        pl.when(i == 4)(lambda: stage1(0))
        return 0

    def z1_copy(i, k):
        return remote(z1s.at[i, k], z1r.at[i, k], z1_ss.at[0], z1_rs.at[i], dev((zp, zm)[k], y, x, c))

    def z1_all(i):
        return remote(z1s.at[i], z1r.at[i], z1_ss.at[0], z1_rs.at[i], sib)

    def z2_copy(i, k):
        return remote(z2s.at[i, k], z2r.at[i, k], z2_ss.at[0], z2_rs.at[i], dev((zp, zm)[k], y, x, c))

    def z2_all(i):
        return remote(z2s.at[i], z2r.at[i], z2_ss.at[0], z2_rs.at[i], sib)

    def y_copy(i, r):
        dy, dc = r // 2, r % 2
        yy, cc = (y + dy) % 4, c + dc - 2 * c * dc
        return remote(ys.at[i, yy * 2 + cc], yr.at[i, r], y_ss.at[0], y_rs.at[i], dev(z, yy, x, cc))

    def y_all(i):
        seven = yr.at[i, 1:8]
        return remote(seven, seven, y_ss.at[0], y_rs.at[i], sib)

    def d_copy(i):
        return remote(ds_.at[i], dr.at[i], d_ss.at[0], d_rs.at[0], dev(z, y, xop, c))

    def block(b):
        return rows16(b * 80, 80)

    def stage1(i):
        x_all(i).wait_recv()
        s_buf[i, :, :256] = s_buf[i, :, :256] + xr[i, 0].astype(f32)
        s_buf[i, :, 256:] = s_buf[i, :, 256:] + xr[i, 1].astype(f32)
        z1s[i, 0] = s_buf[i, block(zo), 0:256].astype(bf16)
        z1s[i, 1] = s_buf[i, block(zo), 256:512].astype(bf16)
        z1_copy(i, 0).start()
        z1_copy(i, 1).start()

    def relay(i):
        z1_all(i).wait_recv()
        z2s[i, 0, :, 0:256] = (s_buf[i, block(zp), 0:256] + z1r[i, 0].astype(f32)).astype(bf16)
        z2s[i, 0, :, 256:512] = s_buf[i, block(zp), 256:512].astype(bf16)
        z2_copy(i, 0).start()
        z2s[i, 1, :, 0:256] = s_buf[i, block(zm), 0:256].astype(bf16)
        z2s[i, 1, :, 256:512] = (s_buf[i, block(zm), 256:512] + z1r[i, 1].astype(f32)).astype(bf16)
        z2_copy(i, 1).start()

    def stage2(i):
        z2_all(i).wait_recv()
        total = s_buf[i, block(z), :] + z2r[i, 0].astype(f32) + z2r[i, 1].astype(f32)
        total = jnp.concatenate([total, jnp.zeros((8, 512), f32)], axis=0)
        for k in range(8):
            piece = total[10 * k : 10 * k + 16, :]
            yf[i, k] = piece
            ys[i, k] = piece.astype(bf16)
        for r in range(1, 8):
            y_copy(i, r).start()

    def stage3(i):
        y_all(i).wait_recv()
        own = yf[i, y * 2 + c]
        for dy in (1, 2, 3):
            own = own + yr[i, 2 * dy].astype(f32)
        other = yr[i, 1].astype(f32)
        for dy in (1, 2, 3):
            other = other + yr[i, 2 * dy + 1].astype(f32)
        ds_[i, 0] = own
        ds_[i, 1] = other
        d_copy(i).start()

    def stage4(i):
        own = (ds_[i, 0] + dr[i, 0]) * scale
        other = (ds_[i, 1] + dr[i, 1]) * scale
        a, n = i // 2, i % 2
        cols = pl.ds(pl.multiple_of(n * 512, 512), 512)
        fin[0, a, :, cols] = jnp.where(mine0, own, other)
        fin[1, a, :, cols] = jnp.where(mine0, other, own)

    lax.fori_loop(0, 6, wg_step, 0)
    stage1(1)
    hook8()
    relay(0)
    inner_all(0).wait_recv()
    z_fwd(2).wait_recv()

    def back1(t, _):
        r = rows16(t * 256, 256)
        v = y_acc[r, :]
        right = jnp.where(col == 15, 0.0, pltpu.roll(v[:, :HALF], 255, 0))
        left = jnp.where(col == 0, 0.0, pltpu.roll(v[:, 2 * HALF : 3 * HALF], 1, 0))
        act_grad = right + v[:, HALF : 2 * HALF] + left
        normed = normed_of(t)
        before = normed * gain + bias
        g = 1.0 / (1.0 + jnp.exp(-before))
        p = act_grad * g * (1.0 + before * (1.0 - g))
        pre[r, :] = p
        s1[pl.ds(t, 1), :] = jnp.sum(p * normed, axis=0, keepdims=True)
        s2[pl.ds(t, 1), :] = jnp.sum(p, axis=0, keepdims=True)
        return 0

    def back2(t, _):
        r = rows16(t * 256, 256)
        v = pre[r, :] * gain - m1[pl.ds(t, 1), :] - normed_of(t) * m2[pl.ds(t, 1), :]
        sgp[t + 1] = (v * inv[pl.ds(t, 1), :]).astype(bf16)
        return 0

    def back1_of(frames):
        for t in frames:
            back1(t, 0)

    def group_terms():
        both = spread_groups(jnp.concatenate([s2[...] * gain, s1[...] * gain], axis=0))
        m1[...] = both[0:8]
        m2[...] = both[8:16]

    halo = [
        remote(hs.at[0], hr.at[0], h_ss.at[0], h_rs.at[0], nxt),
        remote(hs.at[1], hr.at[1], h_ss.at[1], h_rs.at[1], prv),
    ]
    ch_id = lax.broadcasted_iota(jnp.int32, (HALF, 80), 0) + c * HALF
    selm[0] = (ch_id == bwd_ref[...].reshape(1, 80)).astype(f32).astype(bf16)
    selm[1] = (ch_id == fwd_ref[...].reshape(1, 80)).astype(f32).astype(bf16)

    def edge_frames():
        group_terms()
        back2(0, 0)
        back2(7, 0)
        hs[0, :, :80] = dot(sgp[8], selm[0]).astype(bf16)
        hs[1, :, :80] = dot(sgp[1], selm[1]).astype(bf16)
        halo[0].start()
        halo[1].start()

    def act_dot(n, tt):
        cols = pl.ds(n * 512, 512)
        lhs = jnp.concatenate(
            [
                jnp.concatenate([gp[tt * 2 + t, 16 * (2 - a) : 16 * (2 - a) + 256, :] for a in range(3)], axis=1)
                for t in range(2)
            ],
            axis=0,
        )
        rhs = w[:, :, :, cols].reshape(3 * CH, 512)
        y_acc[rows16(tt * 512, 512), cols] = dot(lhs, rhs)

    def act_step(i, _):
        act_dot(0, i)
        plan = {
            0: [(stage1, 2), (relay, 1)],
            1: [(stage2, 0)],
            2: [(stage1, 3)],
            3: [(relay, 2), (stage2, 1)],
        }
        for k in range(4):

            @pl.when(i == k)
            def _(k=k):
                if k == 0:
                    hook_in(2, 1)
                if k == 2:
                    hook_in(3, 1)
                for stage, chunk in plan.get(k, []):
                    stage(chunk)

        return 0

    lax.fori_loop(0, 4, act_step, 0)
    stage1(4)
    inner_all(1).wait_recv()
    z_fwd(3).wait_recv()
    act_dot(1, 3)
    stage1(5)
    relay(3)
    act_dot(1, 0)
    back1_of((6, 7))
    relay(4)
    stage2(2)
    act_dot(1, 1)
    back1_of((0, 1))
    stage3(0)
    edge_frames()
    relay(5)
    act_dot(1, 2)
    stage2(3)
    back1_of((2, 3))
    stage3(1)

    def a1_copy(r):
        dx, dc = r // 2, r % 2
        cc = c + dc - 2 * c * dc
        return remote(a1s, a1r.at[r], a1_ss.at[0], a1_rs.at[0], dev(z, y, (x + dx) % 4, cc))

    def a2_copy(r):
        return remote(a2s, a2r.at[r], a2_ss.at[0], a2_rs.at[0], dev((z + r // 4) % 4, (y + r % 4) % 4, x, c))

    a1_all = remote(a1r.at[1:8], a1r.at[1:8], a1_ss.at[0], a1_rs.at[0], sib)
    a2_all = remote(a2r.at[1:16], a2r.at[1:16], a2_ss.at[0], a2_rs.at[0], sib)

    back1_of((4, 5))
    total = [jnp.sum(v[...], axis=0, keepdims=True) for v in (s1, s2)]
    a1s[:, :HALF] = jnp.concatenate(total + [jnp.zeros((6, HALF), f32)], axis=0)
    for r in range(1, 8):
        a1_copy(r).start()
    stage2(4)
    group_terms()
    lax.fori_loop(1, 7, back2, 0)
    ones = jnp.ones((8, 80), bf16)
    bwd_mask = dot_nt(ones, selm[0])[0:1, :] > 0.5
    fwd_mask = dot_nt(ones, selm[1])[0:1, :] > 0.5

    def shift(t):
        v = jnp.where(bwd_mask, sgp[t].astype(f32), sgp[t + 1].astype(f32))
        return jnp.where(fwd_mask, sgp[t + 2].astype(f32), v)

    def shift_other(i, _):
        igs[i, :, :HALF] = shift(oc * 4 + i).astype(bf16)
        return 0

    lax.fori_loop(c, c + 3, shift_other, 0)
    inside = pl.ds(c, 3)
    i_copies = [
        remote(igs.at[inside], igr.at[inside], ex_s.at[2], ex_r.at[2], sib),
        remote(igs.at[3 * oc], igr.at[3 * oc], ex_s.at[3], ex_r.at[3], sib),
    ]
    i_copies[0].start()
    stage3(2)
    stage2(5)
    halo[0].wait_recv()
    halo[1].wait_recv()
    keep_prev = jnp.where(f >= 2, 1.0, 0.0)
    keep_next = jnp.where(f < 62, 1.0, 0.0)
    sgp[0] = (dot_nt(hr[0, :, :80], selm[0]) * keep_prev).astype(bf16)
    sgp[9] = (dot_nt(hr[1, :, :80], selm[1]) * keep_next).astype(bf16)
    shift_other(3 * oc, 0)
    i_copies[1].start()
    a1_all.wait_recv()
    own = a1s[0:2, :HALF]
    for r in (2, 4, 6):
        own = own + a1r[r, 0:2, :HALF]
    other = a1r[1, 0:2, :HALF]
    for r in (3, 5, 7):
        other = other + a1r[r, 0:2, :HALF]
    a2s[:, :HALF] = jnp.concatenate([own, other, jnp.zeros((4, HALF), f32)], axis=0)
    for r in range(1, 16):
        a2_copy(r).start()
    stage3(3)
    stage3(4)
    stage3(5)
    inner_frames = igr.at[0:3]
    remote(inner_frames, inner_frames, ex_s.at[2], ex_r.at[2], sib).wait_recv()
    i_copies[1].wait_recv()

    def assemble(i, _):
        own = shift(c * 4 + i)
        other = igr[i, :, :HALF].astype(f32)
        v = jnp.concatenate([jnp.where(mine0, own, other), jnp.where(mine0, other, own)], axis=1)
        igo[rows16(i * 256, 256), :] = v.astype(bf16)
        return 0

    lax.fori_loop(0, 4, assemble, 0)
    o_copy = pltpu.make_async_copy(igo, ig_hbm, loc_sem.at[2])
    o_copy.start()

    p1_all(0).wait_send()
    p1_all(1).wait_send()
    for cp in (g_remote, x_remote, *i_copies, halo[0], halo[1]):
        cp.wait_send()
    one, two = w.at[:, 0], w.at[:, 0:2]
    for ref, sem in ((two, zo_s), (one, zf_s), (two, cr_s), (two, yi_s), (wgs, x_s), (z1s, z1_ss), (z2s, z2_ss), (yr.at[:, 1:8], y_ss)):
        remote(ref, ref, sem.at[0], sem.at[0], sib).wait_send()
    a1_all.wait_send()

    remote(ds_, dr, d_ss.at[0], d_rs.at[0], sib).wait_recv()
    for i in range(6):
        stage4(i)
    for a in range(3):
        for b in range(3):
            tap = jnp.concatenate([fin[h, a, 0:10, b * HALF : (b + 1) * HALF] for h in range(2)], axis=1)
            wg_ref[:, (3 * a + b) * CH : (3 * a + b + 1) * CH] = tap
    total = a2s[:, :HALF]
    a2_all.wait_recv()
    for r in range(1, 16):
        total = total + a2r[r, :, :HALF]
    total = total * scale
    own, other = total[0:2, :], total[2:4, :]
    both = jnp.concatenate([jnp.where(mine0, own, other), jnp.where(mine0, other, own)], axis=1)
    gg_ref[...] = both[0:1, :].reshape(CH)
    bg_ref[...] = both[1:2, :].reshape(CH)
    a2_all.wait_send()
    remote(ds_, dr, d_ss.at[0], d_rs.at[0], sib).wait_send()
    o_copy.wait()


def hand_over(ig_in, wg_in, gg_in, bg_in, ig_out, wg_out, gg_out, bg_out, ig, wg, gg, bg, in_sem, out_sem):
    rows = [pl.ds(256 * k, 256) for k in range(4)]
    sets = [(ig_in.at[r], ig.at[r], ig_out.at[r]) for r in rows]
    sets += [(wg_in, wg, wg_out), (gg_in, gg, gg_out), (bg_in, bg, bg_out)]
    first = [pltpu.make_async_copy(a, b, in_sem.at[k]) for k, (a, b, _) in enumerate(sets)]
    second = [pltpu.make_async_copy(b, d, out_sem.at[k]) for k, (_, b, d) in enumerate(sets)]
    for cp in first:
        cp.start()
    for a, b in zip(first, second):
        a.wait()
        b.start()
    for cp in second:
        cp.wait()


def on_device(shifted, out_grad, conv_weight, norm_gain, norm_bias, shift_fwd, shift_bwd):
    scale = 131072.0 ** (-0.5)
    x = shifted.reshape(1024, CH)
    g = out_grad.reshape(4, 256, CH)
    dma = pltpu.SemaphoreType.DMA
    vm = pltpu.VMEM
    scratch = [
        vm((2, 2, 128, 128), bf16), vm((2, 3, 16, WIDE), f32), vm((1024, CH), bf16),
        vm((2, 1024, FULL), bf16), vm((1024, FULL), bf16), vm((8, 288, CH), bf16), vm((CH, 2048), bf16),
        vm((CH, CH), bf16), vm((8, 288, WIDE), bf16), vm((8, 2, 128, 128), bf16), vm((3, 8, 80, WIDE), bf16),
        vm((2048, WIDE), f32), vm((2048, HALF), f32),
        vm((8, HALF), f32), vm((8, HALF), f32), vm((8, HALF), f32), vm((8, HALF), f32), vm((8, HALF), f32), vm((8, HALF), f32),
        vm((6, HALF, 512), f32), vm((6, 2, HALF, 256), bf16), vm((6, 2, HALF, 256), bf16),
        vm((6, 2, 80, 256), bf16), vm((6, 2, 80, 256), bf16), vm((6, 2, 80, 512), bf16), vm((6, 2, 80, 512), bf16),
        vm((6, 8, 16, 512), f32), vm((6, 8, 16, 512), bf16), vm((6, 8, 16, 512), bf16),
        vm((6, 2, 16, 512), f32), vm((6, 2, 16, 512), f32),
        vm((10, 256, HALF), bf16), vm((4, 256, FULL), bf16), vm((4, 256, FULL), bf16), vm((1024, CH), bf16),
        vm((2, 256, 128), bf16), vm((2, 256, 128), bf16), vm((2, HALF, 80), bf16),
        vm((8, FULL), f32), vm((8, 8, FULL), f32), vm((8, FULL), f32), vm((16, 8, FULL), f32),
        dma((4,)), dma((4,)), dma((4,)), dma((2,)), dma((2,)), dma((1,)), dma((4,)), dma((1,)), dma((4,)),
        dma((1,)), dma((4, 2)), dma((1,)), dma((2,)),
        dma((1,)), dma((6,)), dma((1,)), dma((6,)), dma((1,)), dma((6,)), dma((1,)), dma((6,)),
        dma((1,)), dma((1,)), dma((2,)), dma((2,)), dma((1,)), dma((1,)), dma((1,)), dma((1,)),
    ]
    v = pl.BlockSpec(memory_space=pltpu.VMEM)

    def body(*refs):
        kernel(scale, *refs)

    shapes = (
        jax.ShapeDtypeStruct((1024, CH), bf16),
        jax.ShapeDtypeStruct((10, 9 * CH), f32),
        jax.ShapeDtypeStruct((CH,), f32),
        jax.ShapeDtypeStruct((CH,), f32),
    )
    anywhere = pl.BlockSpec(memory_space=pl.ANY)
    parts = pl.pallas_call(
        body,
        out_shape=shapes,
        in_specs=[pl.BlockSpec(memory_space=pl.ANY), pl.BlockSpec(memory_space=pl.ANY), v, v, v, v, v],
        out_specs=(anywhere, v, v, v),
        scratch_shapes=scratch,
        compiler_params=pltpu.CompilerParams(collective_id=0, has_side_effects=True, vmem_limit_bytes=60 << 20),
    )(x, g, conv_weight, norm_gain, norm_bias, shift_fwd, shift_bwd)
    ig, wg, gg, bg = pl.pallas_call(
        hand_over,
        out_shape=shapes,
        in_specs=[anywhere] * 4,
        out_specs=(anywhere,) * 4,
        scratch_shapes=[
            vm((1024, CH), bf16), vm((10, 9 * CH), f32), vm((CH,), f32), vm((CH,), f32), dma((7,)), dma((7,)),
        ],
    )(*parts)
    return (ig.reshape(shifted.shape), wg, gg, bg)


def solution(mesh):
    in_specs = (
        P("dp", "frames", None, None, None),
        P("dp", "frames", None, None, None),
        P("frames", None),
        P(),
        P(),
        P(),
        P(),
    )
    out_specs = (P("dp", "frames", None, None, None), P("frames", None), P(), P())
    return jax.shard_map(
        on_device, mesh=mesh, in_specs=in_specs, out_specs=out_specs, check_vma=False
    )
```

```python
import jax
import jax.numpy as jnp
from jax import lax
from jax.experimental import pallas as pl
from jax.experimental.pallas import tpu as pltpu
from jax.sharding import PartitionSpec as P

f32, bf16 = jnp.float32, jnp.bfloat16
MESH = pl.DeviceIdType.MESH
EPS = 1e-05
CH, HALF, WIDE = 640, 320, 1024
FULL = 384
HIGH = lax.Precision.HIGHEST


def dot(a, b):
    return jnp.dot(a, b, preferred_element_type=f32)


def dot_nt(a, b):
    return lax.dot_general(a, b, (((1,), (1,)), ((), ())), preferred_element_type=f32)


def rows16(v, n):
    return pl.ds(pl.multiple_of(v, 16), n)


def div20(i):
    return (i * 3277) >> 16


def kernel(
    scale,
    x_hbm, g_hbm, w_ref, gain_ref, bias_ref, fwd_ref, bwd_ref,
    ig_hbm, wg_ref, gg_ref, bg_ref,
    wpc, fin, x_ref, xs, xb, gp, gt, pm, ap, p1, w, y_acc, pre,
    cen, inv, s1, s2, m1, m2,
    s_buf, wgs, xr, z1s, z1r, z2s, z2r, yf, ys, yr, ds_, dr,
    sgp, igs, igr, igo, hs, hr, selm, a1s, a1r, a2s, a2r,
    loc_sem, ex_s, ex_r, p1_s, p1_r, zo_s, zo_r, zf_s, zf_r, cr_s, cr_r, yi_s, yi_r,
    x_s, x_r, z1_ss, z1_rs, z2_ss, z2_rs, y_ss, y_rs, d_ss, d_rs, h_ss, h_rs, a1_ss, a1_rs, a2_ss, a2_rs,
):
    f = lax.axis_index("frames")
    d = lax.axis_index("dp")
    c = f % 2
    xl = (f // 2) % 2
    y = (f // 4) % 4
    z = f // 16
    x = d * 2 + xl
    y0 = y % 2
    y1 = y // 2

    def dev(zz, yy, xx, cc):
        return {"frames": ((zz * 4 + yy) * 2 + xx % 2) * 2 + cc, "dp": xx // 2}

    oc = 1 - c
    zp, zm, zo = (z + 1) % 4, (z + 3) % 4, (z + 2) % 4
    yin = y + 1 - 2 * y0
    ycross = (y + 3 + 2 * y0) % 4
    xin = x + 1 - 2 * xl
    xcross = (x + 3 + 2 * xl) % 4
    xop = (x + 2) % 4
    sib = dev(z, y, x, oc)
    nxt = {"frames": (f + 2) % 64, "dp": d}
    prv = {"frames": (f + 62) % 64, "dp": d}

    def remote(src, dst, ss, rs, to):
        return pltpu.make_async_remote_copy(
            src_ref=src, dst_ref=dst, send_sem=ss, recv_sem=rs, device_id=to, device_id_type=MESH
        )

    barrier = pltpu.get_barrier_semaphore()
    partners = [sib, nxt, prv]
    for yy, xx in ((yin, x), (y, xin), (yin, xin)):
        partners += [dev(z, yy, xx, 0), dev(z, yy, xx, 1)]
    for k in (2, 3):
        yy = (ycross, (y + 2) % 4)[k - 2]
        partners += [dev(z, yy, x, 0), dev(z, yy, x, 1)]
    for xx in (xcross, xop):
        partners += [dev(z, y, xx, 0), dev(z, y, xx, 1)]
    partners += [dev(zz, (y + dy) % 4, x, c) for zz in (zp, zm, zo) for dy in range(4)]
    for to in partners:
        pl.semaphore_signal(barrier, inc=1, device_id=to, device_id_type=MESH)

    x_local = pltpu.make_async_copy(x_hbm, x_ref, loc_sem.at[1])
    x_local.start()
    for h in range(2):
        wide = []
        for a in range(3):
            taps = [w_ref[:, (3 * a + b) * CH + h * HALF : (3 * a + b) * CH + (h + 1) * HALF].astype(f32) for b in range(3)]
            wide.append(jnp.concatenate(taps + [jnp.zeros((10, WIDE - 3 * HALF), f32)], axis=1))
        for half in range(2):
            pieces = [wide[a][:, lb * 128 : lb * 128 + 128] for lb in range(4 * half, 4 * half + 4) for a in range(3)]
            wpc[h, half] = jnp.concatenate(pieces + [jnp.zeros((8, 128), f32)], axis=0).astype(bf16)
    pl.semaphore_wait(barrier, len(partners))
    me8 = (y0 * 2 + xl) * 2 + c
    def p1_all(half):
        seven = p1.at[0:7, half]
        return remote(seven, seven, p1_s.at[half], p1_r.at[half], sib)

    p1c = ([], [])
    for half in range(2):
        k = 0
        for yy, xx, dc in ((yin, xin, 0), (yin, xin, 1), (yin, x, 0), (yin, x, 1), (y, xin, 0), (y, xin, 1), (y, x, 1)):
            cc = c + dc - 2 * c * dc
            to = dev(z, yy, xx, cc)
            p1c[half].append(remote(wpc.at[cc, half], p1.at[me8, half], p1_s.at[half], p1_r.at[half], to))
            k += 1
    for cp in p1c[0]:
        cp.start()
    interior = (pl.ds(c * 4, 4), pl.ds(16, 256))
    g_local = pltpu.make_async_copy(g_hbm, gp.at[interior], loc_sem.at[0])
    g_remote = remote(g_hbm, gp.at[interior], ex_s.at[0], ex_r.at[0], sib)
    g_local.start()
    p1[me8] = wpc[c]

    x_local.wait()
    def split(t, _):
        r = rows16(t * 256, 256)
        v = x_ref[r, :].astype(f32)
        xs[0, r, :HALF] = v[:, :HALF].astype(bf16)
        xs[1, r, :HALF] = v[:, HALF:].astype(bf16)
        return 0

    lax.fori_loop(0, 4, split, 0)
    x_remote = remote(xs.at[oc], xb, ex_s.at[1], ex_r.at[1], sib)
    x_remote.start()
    g_remote.start()

    def read_x(t):
        r = rows16((t % 4) * 256, 256)
        mine = xs[c, r, :HALF]
        other = xb[r, :HALF]
        return jnp.where(t // 4 == c, mine, other).astype(f32)

    zero16 = jnp.zeros((16, CH), bf16)
    zero16w = jnp.zeros((16, WIDE), bf16)
    for t in range(8):
        gp[t, 0:16, :] = zero16
        gp[t, 272:288, :] = zero16
        ap[t, 0:16, :] = zero16w
        ap[t, 272:288, :] = zero16w

    oi = lax.broadcasted_iota(jnp.int32, (CH, CH), 0)
    li = lax.broadcasted_iota(jnp.int32, (CH, CH), 1)
    q = (oi >= HALF).astype(jnp.int32)
    rr = oi - HALF * q
    zy = div20(rr)
    src_row = (2 * zy + (q + xl - 2 * q * xl)) * 20 + (rr - 20 * zy)
    pm[...] = (li == src_row).astype(f32).astype(bf16)
    gi = div20(lax.broadcasted_iota(jnp.int32, (HALF, HALF), 0))
    gj = div20(lax.broadcasted_iota(jnp.int32, (HALF, HALF), 1))
    group_mean = jnp.where(gi == gj, 1.0 / 5120.0, 0.0).astype(f32)

    def spread_groups(v):
        return jnp.dot(v, group_mean, preferred_element_type=f32, precision=HIGH)

    mine0 = c == 0
    gain_all, bias_all = gain_ref[...].reshape(1, CH), bias_ref[...].reshape(1, CH)
    gain = jnp.where(mine0, gain_all[:, :HALF], gain_all[:, HALF:])
    bias = jnp.where(mine0, bias_all[:, :HALF], bias_all[:, HALF:])

    def transpose(t):
        gt[:, pl.ds(pl.multiple_of(t * 256, 256), 256)] = dot_nt(pm[...], gp[t, 16:272, :]).astype(bf16)

    g_local.wait()

    def transpose_mine(i, _):
        transpose(c * 4 + i)
        return 0

    lax.fori_loop(0, 4, transpose_mine, 0)
    for cp in p1c[1]:
        cp.start()

    x_remote.wait_recv()

    def stat_sum(t, _):
        s1[pl.ds(t, 1), :] = jnp.sum(read_x(t), axis=0, keepdims=True)
        return 0

    lax.fori_loop(0, 8, stat_sum, 0)
    cen[...] = spread_groups(s1[...])

    def stat_sq(t, _):
        v = read_x(t) - cen[pl.ds(t, 1), :]
        s2[pl.ds(t, 1), :] = jnp.sum(v * v, axis=0, keepdims=True)
        return 0

    lax.fori_loop(0, 8, stat_sq, 0)
    inv[...] = lax.rsqrt(spread_groups(s2[...]) + EPS)

    blk = z * 2 + y1

    def dense(half):
        p1_all(half).wait_recv()
        for lb in range(4):
            for a in range(3):
                r = (lb * 3 + a) * 10
                piece = jnp.concatenate([p1[s, half, r : r + 10, :].astype(f32) for s in range(8)], axis=0)
                at = (half * 4 + lb) * 128
                w[a, blk, :, at : at + 128] = piece.astype(bf16)

    dense(0)

    def lanes(qq, n=256):
        return pl.ds(pl.multiple_of(qq * 256, 256), n)

    def wsl(b, qq):
        return w.at[:, b, :, lanes(qq)]

    def quarter(j):
        return (2 * (j % 2) + 1 - y0) if j < 2 else (2 * (j % 2) + y0)

    def z_own(k, j):
        s = wsl(blk, quarter(j))
        return remote(s, s, zo_s.at[0], zo_r.at[j], dev((zp, zm)[k], y, x, c))

    def z_fwd(j):
        up = j % 2 == 0
        s = wsl((zm if up else zp) * 2 + y1, quarter(j))
        return remote(s, s, zf_s.at[0], zf_r.at[j], dev(zp if up else zm, y, x, c))

    zrel = (z, zm, zp, zo)

    def cross(k, h):
        s = wsl(zrel[k] * 2 + y1, 2 * h + 1 - y0)
        return remote(s, s, cr_s.at[0], cr_r.at[k, h], dev(z, ycross, x, c))

    def inner(k, h):
        s = wsl(zrel[k] * 2 + 1 - y1, 2 * h + y0)
        return remote(s, s, yi_s.at[0], yi_r.at[h], dev(z, yin, x, c))

    def inner_all(h):
        one = w.at[:, 0]
        return remote(one, one, yi_s.at[0], yi_r.at[h], sib)

    def z_start(j):
        z_own(0, j).start()
        z_own(1, j).start()

    def z_wait(j):
        two = w.at[:, 0:2, :, 0:256]
        remote(two, two, zo_s.at[0], zo_r.at[j], sib).wait_recv()

    def hook_in(k, h):
        cross(k, h).wait_recv()
        inner(k, h).start()

    def hook0():
        dense(1)
        z_start(1)
        cross(0, 1).start()

    def hook1():
        z_wait(0)
        z_fwd(0).start()
        cross(1, 0).start()
        hook_in(0, 0)
        z_start(2)

    def hook2():
        cross(2, 0).start()

    def hook3():
        z_wait(1)
        z_fwd(1).start()
        hook_in(0, 1)
        z_start(3)

    def hook4():
        z_fwd(0).wait_recv()
        cross(3, 0).start()
        hook_in(1, 0)

    def hook5():
        cross(1, 1).start()
        z_wait(2)
        z_fwd(2).start()

    def hook6():
        hook_in(2, 0)
        z_fwd(1).wait_recv()
        cross(2, 1).start()

    def hook7():
        hook_in(3, 0)
        cross(3, 1).start()

    def hook8():
        hook_in(1, 1)
        z_wait(3)
        z_fwd(3).start()

    cross(0, 0).start()
    z_start(0)

    col = lax.broadcasted_iota(jnp.int32, (256, HALF), 0) % 16

    def normed_of(t):
        return (read_x(t) - cen[pl.ds(t, 1), :]) * inv[pl.ds(t, 1), :]

    def forward(t, _):
        before = normed_of(t) * gain + bias
        act = before / (1.0 + jnp.exp(-before))
        left = jnp.where(col == 0, 0.0, pltpu.roll(act, 1, 0))
        right = jnp.where(col == 15, 0.0, pltpu.roll(act, 255, 0))
        cat = jnp.concatenate([left, act, right, jnp.zeros((256, WIDE - 3 * HALF), f32)], axis=1)
        ap[t, 16:272, :] = cat.astype(bf16)
        return 0

    g_remote.wait_recv()

    def forward_pair(i, _):
        transpose(oc * 4 + i)
        forward(2 * i, 0)
        forward(2 * i + 1, 0)
        pl.when(i == 1)(hook0)
        return 0

    lax.fori_loop(0, 4, forward_pair, 0)
    hook1()

    def x_copy(i, k):
        to = (xin, xcross)[k]
        return remote(wgs.at[i, k], xr.at[i, k], x_s.at[0], x_r.at[i], dev(z, y, to, c))

    def x_all(i):
        return remote(wgs.at[i], xr.at[i], x_s.at[0], x_r.at[i], sib)

    def wg_step(i, _):
        a, n = i // 2, i % 2
        cols = pl.ds(pl.multiple_of(n * 512, 512), 512)
        acc = None
        for t in range(8):
            v = dot(gt[:, t * 256 : t * 256 + 256], ap[t, rows16(a * 16, 256), cols])
            acc = v if acc is None else acc + v
        s_buf[i] = acc[:HALF, :]
        wgs[i, 0] = acc[HALF:, :256].astype(bf16)
        wgs[i, 1] = acc[HALF:, 256:].astype(bf16)
        x_copy(i, 0).start()
        x_copy(i, 1).start()

        for k, hook in enumerate((hook2, hook3, hook4, hook5, hook6, hook7)):
            pl.when(i == k)(hook)
        pl.when(i == 4)(lambda: stage1(0))
        return 0

    def z1_copy(i, k):
        return remote(z1s.at[i, k], z1r.at[i, k], z1_ss.at[0], z1_rs.at[i], dev((zp, zm)[k], y, x, c))

    def z1_all(i):
        return remote(z1s.at[i], z1r.at[i], z1_ss.at[0], z1_rs.at[i], sib)

    def z2_copy(i, k):
        return remote(z2s.at[i, k], z2r.at[i, k], z2_ss.at[0], z2_rs.at[i], dev((zp, zm)[k], y, x, c))

    def z2_all(i):
        return remote(z2s.at[i], z2r.at[i], z2_ss.at[0], z2_rs.at[i], sib)

    def y_copy(i, r):
        dy, dc = r // 2, r % 2
        yy, cc = (y + dy) % 4, c + dc - 2 * c * dc
        return remote(ys.at[i, yy * 2 + cc], yr.at[i, r], y_ss.at[0], y_rs.at[i], dev(z, yy, x, cc))

    def y_all(i):
        seven = yr.at[i, 1:8]
        return remote(seven, seven, y_ss.at[0], y_rs.at[i], sib)

    def d_copy(i):
        return remote(ds_.at[i], dr.at[i], d_ss.at[0], d_rs.at[0], dev(z, y, xop, c))

    def block(b):
        return rows16(b * 80, 80)

    def stage1(i):
        x_all(i).wait_recv()
        s_buf[i, :, :256] = s_buf[i, :, :256] + xr[i, 0].astype(f32)
        s_buf[i, :, 256:] = s_buf[i, :, 256:] + xr[i, 1].astype(f32)
        z1s[i, 0] = s_buf[i, block(zo), 0:256].astype(bf16)
        z1s[i, 1] = s_buf[i, block(zo), 256:512].astype(bf16)
        z1_copy(i, 0).start()
        z1_copy(i, 1).start()

    def relay(i):
        z1_all(i).wait_recv()
        z2s[i, 0, :, 0:256] = (s_buf[i, block(zp), 0:256] + z1r[i, 0].astype(f32)).astype(bf16)
        z2s[i, 0, :, 256:512] = s_buf[i, block(zp), 256:512].astype(bf16)
        z2_copy(i, 0).start()
        z2s[i, 1, :, 0:256] = s_buf[i, block(zm), 0:256].astype(bf16)
        z2s[i, 1, :, 256:512] = (s_buf[i, block(zm), 256:512] + z1r[i, 1].astype(f32)).astype(bf16)
        z2_copy(i, 1).start()

    def stage2(i):
        z2_all(i).wait_recv()
        total = s_buf[i, block(z), :] + z2r[i, 0].astype(f32) + z2r[i, 1].astype(f32)
        total = jnp.concatenate([total, jnp.zeros((8, 512), f32)], axis=0)
        for k in range(8):
            piece = total[10 * k : 10 * k + 16, :]
            yf[i, k] = piece
            ys[i, k] = piece.astype(bf16)
        for r in range(1, 8):
            y_copy(i, r).start()

    def stage3(i):
        y_all(i).wait_recv()
        own = yf[i, y * 2 + c]
        for dy in (1, 2, 3):
            own = own + yr[i, 2 * dy].astype(f32)
        other = yr[i, 1].astype(f32)
        for dy in (1, 2, 3):
            other = other + yr[i, 2 * dy + 1].astype(f32)
        ds_[i, 0] = own
        ds_[i, 1] = other
        d_copy(i).start()

    def stage4(i):
        own = (ds_[i, 0] + dr[i, 0]) * scale
        other = (ds_[i, 1] + dr[i, 1]) * scale
        a, n = i // 2, i % 2
        cols = pl.ds(pl.multiple_of(n * 512, 512), 512)
        fin[0, a, :, cols] = jnp.where(mine0, own, other)
        fin[1, a, :, cols] = jnp.where(mine0, other, own)

    lax.fori_loop(0, 6, wg_step, 0)
    stage1(1)
    hook8()
    relay(0)
    inner_all(0).wait_recv()
    z_fwd(2).wait_recv()

    def back1(t, _):
        r = rows16(t * 256, 256)
        v = y_acc[r, :]
        right = jnp.where(col == 15, 0.0, pltpu.roll(v[:, :HALF], 255, 0))
        left = jnp.where(col == 0, 0.0, pltpu.roll(v[:, 2 * HALF : 3 * HALF], 1, 0))
        act_grad = right + v[:, HALF : 2 * HALF] + left
        normed = normed_of(t)
        before = normed * gain + bias
        g = 1.0 / (1.0 + jnp.exp(-before))
        p = act_grad * g * (1.0 + before * (1.0 - g))
        pre[r, :] = p
        s1[pl.ds(t, 1), :] = jnp.sum(p * normed, axis=0, keepdims=True)
        s2[pl.ds(t, 1), :] = jnp.sum(p, axis=0, keepdims=True)
        return 0

    def back2(t, _):
        r = rows16(t * 256, 256)
        v = pre[r, :] * gain - m1[pl.ds(t, 1), :] - normed_of(t) * m2[pl.ds(t, 1), :]
        sgp[t + 1] = (v * inv[pl.ds(t, 1), :]).astype(bf16)
        return 0

    def back1_of(frames):
        for t in frames:
            back1(t, 0)

    def group_terms():
        both = spread_groups(jnp.concatenate([s2[...] * gain, s1[...] * gain], axis=0))
        m1[...] = both[0:8]
        m2[...] = both[8:16]

    halo = [
        remote(hs.at[0], hr.at[0], h_ss.at[0], h_rs.at[0], nxt),
        remote(hs.at[1], hr.at[1], h_ss.at[1], h_rs.at[1], prv),
    ]
    ch_id = lax.broadcasted_iota(jnp.int32, (HALF, 80), 0) + c * HALF
    selm[0] = (ch_id == bwd_ref[...].reshape(1, 80)).astype(f32).astype(bf16)
    selm[1] = (ch_id == fwd_ref[...].reshape(1, 80)).astype(f32).astype(bf16)

    def edge_frames():
        group_terms()
        back2(0, 0)
        back2(7, 0)
        hs[0, :, :80] = dot(sgp[8], selm[0]).astype(bf16)
        hs[1, :, :80] = dot(sgp[1], selm[1]).astype(bf16)
        halo[0].start()
        halo[1].start()

    def act_dot(n, tt):
        cols = pl.ds(n * 512, 512)
        lhs = jnp.concatenate(
            [
                jnp.concatenate([gp[tt * 2 + t, 16 * (2 - a) : 16 * (2 - a) + 256, :] for a in range(3)], axis=1)
                for t in range(2)
            ],
            axis=0,
        )
        rhs = w[:, :, :, cols].reshape(3 * CH, 512)
        y_acc[rows16(tt * 512, 512), cols] = dot(lhs, rhs)

    def act_step(i, _):
        act_dot(0, i)
        plan = {
            0: [(stage1, 2), (relay, 1)],
            1: [(stage2, 0)],
            2: [(stage1, 3)],
            3: [(relay, 2), (stage2, 1)],
        }
        for k in range(4):

            @pl.when(i == k)
            def _(k=k):
                if k == 0:
                    hook_in(2, 1)
                for stage, chunk in plan.get(k, []):
                    stage(chunk)
                if k == 1:
                    hook_in(3, 1)

        return 0

    lax.fori_loop(0, 4, act_step, 0)
    stage1(4)
    inner_all(1).wait_recv()
    z_fwd(3).wait_recv()
    act_dot(1, 3)
    stage1(5)
    relay(3)
    act_dot(1, 0)
    back1_of((6, 7))
    relay(4)
    stage2(2)
    act_dot(1, 1)
    back1_of((0, 1))
    stage3(0)
    edge_frames()
    relay(5)
    act_dot(1, 2)
    stage2(3)
    back1_of((2, 3))
    stage3(1)

    def a1_copy(r):
        dx, dc = r // 2, r % 2
        cc = c + dc - 2 * c * dc
        return remote(a1s, a1r.at[r], a1_ss.at[0], a1_rs.at[0], dev(z, y, (x + dx) % 4, cc))

    def a2_copy(r):
        return remote(a2s, a2r.at[r], a2_ss.at[0], a2_rs.at[0], dev((z + r // 4) % 4, (y + r % 4) % 4, x, c))

    a1_all = remote(a1r.at[1:8], a1r.at[1:8], a1_ss.at[0], a1_rs.at[0], sib)
    a2_all = remote(a2r.at[1:16], a2r.at[1:16], a2_ss.at[0], a2_rs.at[0], sib)

    back1_of((4, 5))
    total = [jnp.sum(v[...], axis=0, keepdims=True) for v in (s1, s2)]
    a1s[:, :HALF] = jnp.concatenate(total + [jnp.zeros((6, HALF), f32)], axis=0)
    for r in range(1, 8):
        a1_copy(r).start()
    stage2(4)
    group_terms()
    lax.fori_loop(1, 7, back2, 0)
    ones = jnp.ones((8, 80), bf16)
    bwd_mask = dot_nt(ones, selm[0])[0:1, :] > 0.5
    fwd_mask = dot_nt(ones, selm[1])[0:1, :] > 0.5

    def shift(t):
        v = jnp.where(bwd_mask, sgp[t].astype(f32), sgp[t + 1].astype(f32))
        return jnp.where(fwd_mask, sgp[t + 2].astype(f32), v)

    def shift_other(i, _):
        igs[i, :, :HALF] = shift(oc * 4 + i).astype(bf16)
        return 0

    lax.fori_loop(c, c + 3, shift_other, 0)
    inside = pl.ds(c, 3)
    i_copies = [
        remote(igs.at[inside], igr.at[inside], ex_s.at[2], ex_r.at[2], sib),
        remote(igs.at[3 * oc], igr.at[3 * oc], ex_s.at[3], ex_r.at[3], sib),
    ]
    i_copies[0].start()
    stage3(2)
    stage2(5)
    halo[0].wait_recv()
    halo[1].wait_recv()
    keep_prev = jnp.where(f >= 2, 1.0, 0.0)
    keep_next = jnp.where(f < 62, 1.0, 0.0)
    sgp[0] = (dot_nt(hr[0, :, :80], selm[0]) * keep_prev).astype(bf16)
    sgp[9] = (dot_nt(hr[1, :, :80], selm[1]) * keep_next).astype(bf16)
    shift_other(3 * oc, 0)
    i_copies[1].start()
    a1_all.wait_recv()
    own = a1s[0:2, :HALF]
    for r in (2, 4, 6):
        own = own + a1r[r, 0:2, :HALF]
    other = a1r[1, 0:2, :HALF]
    for r in (3, 5, 7):
        other = other + a1r[r, 0:2, :HALF]
    a2s[:, :HALF] = jnp.concatenate([own, other, jnp.zeros((4, HALF), f32)], axis=0)
    for r in range(1, 16):
        a2_copy(r).start()
    stage3(3)
    stage3(4)
    stage3(5)
    inner_frames = igr.at[0:3]
    remote(inner_frames, inner_frames, ex_s.at[2], ex_r.at[2], sib).wait_recv()
    i_copies[1].wait_recv()

    def assemble(i, _):
        own = shift(c * 4 + i)
        other = igr[i, :, :HALF].astype(f32)
        v = jnp.concatenate([jnp.where(mine0, own, other), jnp.where(mine0, other, own)], axis=1)
        igo[rows16(i * 256, 256), :] = v.astype(bf16)
        return 0

    lax.fori_loop(0, 4, assemble, 0)
    o_copy = pltpu.make_async_copy(igo, ig_hbm, loc_sem.at[2])
    o_copy.start()

    p1_all(0).wait_send()
    p1_all(1).wait_send()
    for cp in (g_remote, x_remote, *i_copies, halo[0], halo[1]):
        cp.wait_send()
    one, two = w.at[:, 0], w.at[:, 0:2]
    for ref, sem in ((two, zo_s), (one, zf_s), (two, cr_s), (two, yi_s), (wgs, x_s), (z1s, z1_ss), (z2s, z2_ss), (yr.at[:, 1:8], y_ss)):
        remote(ref, ref, sem.at[0], sem.at[0], sib).wait_send()
    a1_all.wait_send()

    remote(ds_, dr, d_ss.at[0], d_rs.at[0], sib).wait_recv()
    for i in range(6):
        stage4(i)
    for a in range(3):
        for b in range(3):
            tap = jnp.concatenate([fin[h, a, 0:10, b * HALF : (b + 1) * HALF] for h in range(2)], axis=1)
            wg_ref[:, (3 * a + b) * CH : (3 * a + b + 1) * CH] = tap
    total = a2s[:, :HALF]
    a2_all.wait_recv()
    for r in range(1, 16):
        total = total + a2r[r, :, :HALF]
    total = total * scale
    own, other = total[0:2, :], total[2:4, :]
    both = jnp.concatenate([jnp.where(mine0, own, other), jnp.where(mine0, other, own)], axis=1)
    gg_ref[...] = both[0:1, :].reshape(CH)
    bg_ref[...] = both[1:2, :].reshape(CH)
    a2_all.wait_send()
    remote(ds_, dr, d_ss.at[0], d_rs.at[0], sib).wait_send()
    o_copy.wait()


def hand_over(ig_in, wg_in, gg_in, bg_in, ig_out, wg_out, gg_out, bg_out, ig, wg, gg, bg, in_sem, out_sem):
    rows = [pl.ds(256 * k, 256) for k in range(4)]
    sets = [(ig_in.at[r], ig.at[r], ig_out.at[r]) for r in rows]
    sets += [(wg_in, wg, wg_out), (gg_in, gg, gg_out), (bg_in, bg, bg_out)]
    first = [pltpu.make_async_copy(a, b, in_sem.at[k]) for k, (a, b, _) in enumerate(sets)]
    second = [pltpu.make_async_copy(b, d, out_sem.at[k]) for k, (_, b, d) in enumerate(sets)]
    for cp in first:
        cp.start()
    for a, b in zip(first, second):
        a.wait()
        b.start()
    for cp in second:
        cp.wait()


def on_device(shifted, out_grad, conv_weight, norm_gain, norm_bias, shift_fwd, shift_bwd):
    scale = 131072.0 ** (-0.5)
    x = shifted.reshape(1024, CH)
    g = out_grad.reshape(4, 256, CH)
    dma = pltpu.SemaphoreType.DMA
    vm = pltpu.VMEM
    scratch = [
        vm((2, 2, 128, 128), bf16), vm((2, 3, 16, WIDE), f32), vm((1024, CH), bf16),
        vm((2, 1024, FULL), bf16), vm((1024, FULL), bf16), vm((8, 288, CH), bf16), vm((CH, 2048), bf16),
        vm((CH, CH), bf16), vm((8, 288, WIDE), bf16), vm((8, 2, 128, 128), bf16), vm((3, 8, 80, WIDE), bf16),
        vm((2048, WIDE), f32), vm((2048, HALF), f32),
        vm((8, HALF), f32), vm((8, HALF), f32), vm((8, HALF), f32), vm((8, HALF), f32), vm((8, HALF), f32), vm((8, HALF), f32),
        vm((6, HALF, 512), f32), vm((6, 2, HALF, 256), bf16), vm((6, 2, HALF, 256), bf16),
        vm((6, 2, 80, 256), bf16), vm((6, 2, 80, 256), bf16), vm((6, 2, 80, 512), bf16), vm((6, 2, 80, 512), bf16),
        vm((6, 8, 16, 512), f32), vm((6, 8, 16, 512), bf16), vm((6, 8, 16, 512), bf16),
        vm((6, 2, 16, 512), f32), vm((6, 2, 16, 512), f32),
        vm((10, 256, HALF), bf16), vm((4, 256, FULL), bf16), vm((4, 256, FULL), bf16), vm((1024, CH), bf16),
        vm((2, 256, 128), bf16), vm((2, 256, 128), bf16), vm((2, HALF, 80), bf16),
        vm((8, FULL), f32), vm((8, 8, FULL), f32), vm((8, FULL), f32), vm((16, 8, FULL), f32),
        dma((4,)), dma((4,)), dma((4,)), dma((2,)), dma((2,)), dma((1,)), dma((4,)), dma((1,)), dma((4,)),
        dma((1,)), dma((4, 2)), dma((1,)), dma((2,)),
        dma((1,)), dma((6,)), dma((1,)), dma((6,)), dma((1,)), dma((6,)), dma((1,)), dma((6,)),
        dma((1,)), dma((1,)), dma((2,)), dma((2,)), dma((1,)), dma((1,)), dma((1,)), dma((1,)),
    ]
    v = pl.BlockSpec(memory_space=pltpu.VMEM)

    def body(*refs):
        kernel(scale, *refs)

    shapes = (
        jax.ShapeDtypeStruct((1024, CH), bf16),
        jax.ShapeDtypeStruct((10, 9 * CH), f32),
        jax.ShapeDtypeStruct((CH,), f32),
        jax.ShapeDtypeStruct((CH,), f32),
    )
    anywhere = pl.BlockSpec(memory_space=pl.ANY)
    parts = pl.pallas_call(
        body,
        out_shape=shapes,
        in_specs=[pl.BlockSpec(memory_space=pl.ANY), pl.BlockSpec(memory_space=pl.ANY), v, v, v, v, v],
        out_specs=(anywhere, v, v, v),
        scratch_shapes=scratch,
        compiler_params=pltpu.CompilerParams(collective_id=0, has_side_effects=True, vmem_limit_bytes=60 << 20),
    )(x, g, conv_weight, norm_gain, norm_bias, shift_fwd, shift_bwd)
    ig, wg, gg, bg = pl.pallas_call(
        hand_over,
        out_shape=shapes,
        in_specs=[anywhere] * 4,
        out_specs=(anywhere,) * 4,
        scratch_shapes=[
            vm((1024, CH), bf16), vm((10, 9 * CH), f32), vm((CH,), f32), vm((CH,), f32), dma((7,)), dma((7,)),
        ],
    )(*parts)
    return (ig.reshape(shifted.shape), wg, gg, bg)


def solution(mesh):
    in_specs = (
        P("dp", "frames", None, None, None),
        P("dp", "frames", None, None, None),
        P("frames", None),
        P(),
        P(),
        P(),
        P(),
    )
    out_specs = (P("dp", "frames", None, None, None), P("frames", None), P(), P())
    return jax.shard_map(
        on_device, mesh=mesh, in_specs=in_specs, out_specs=out_specs, check_vma=False
    )
```

```python
import jax
import jax.numpy as jnp
from jax import lax
from jax.experimental import pallas as pl
from jax.experimental.pallas import tpu as pltpu
from jax.sharding import PartitionSpec as P

f32, bf16 = jnp.float32, jnp.bfloat16
MESH = pl.DeviceIdType.MESH
EPS = 1e-05
CH, HALF, WIDE = 640, 320, 1024
FULL = 384
HIGH = lax.Precision.HIGHEST


def dot(a, b):
    return jnp.dot(a, b, preferred_element_type=f32)


def dot_nt(a, b):
    return lax.dot_general(a, b, (((1,), (1,)), ((), ())), preferred_element_type=f32)


def rows16(v, n):
    return pl.ds(pl.multiple_of(v, 16), n)


def div20(i):
    return (i * 3277) >> 16


def kernel(
    scale,
    x_hbm, g_hbm, w_ref, gain_ref, bias_ref, fwd_ref, bwd_ref,
    ig_hbm, wg_ref, gg_ref, bg_ref,
    wpc, fin, x_ref, xs, xb, gp, gt, pm, ap, p1, w, y_acc, pre,
    cen, inv, s1, s2, m1, m2,
    s_buf, wgs, xr, z1s, z1r, z2s, z2r, yf, ys, yr, ds_, dr,
    sgp, igs, igr, igo, hs, hr, selm, a1s, a1r, a2s, a2r,
    loc_sem, ex_s, ex_r, p1_s, p1_r, zo_s, zo_r, zf_s, zf_r, cr_s, cr_r, yi_s, yi_r,
    x_s, x_r, z1_ss, z1_rs, z2_ss, z2_rs, y_ss, y_rs, d_ss, d_rs, h_ss, h_rs, a1_ss, a1_rs, a2_ss, a2_rs,
):
    f = lax.axis_index("frames")
    d = lax.axis_index("dp")
    c = f % 2
    xl = (f // 2) % 2
    y = (f // 4) % 4
    z = f // 16
    x = d * 2 + xl
    y0 = y % 2
    y1 = y // 2

    def dev(zz, yy, xx, cc):
        return {"frames": ((zz * 4 + yy) * 2 + xx % 2) * 2 + cc, "dp": xx // 2}

    oc = 1 - c
    zp, zm, zo = (z + 1) % 4, (z + 3) % 4, (z + 2) % 4
    yin = y + 1 - 2 * y0
    ycross = (y + 3 + 2 * y0) % 4
    xin = x + 1 - 2 * xl
    xcross = (x + 3 + 2 * xl) % 4
    xop = (x + 2) % 4
    sib = dev(z, y, x, oc)
    nxt = {"frames": (f + 2) % 64, "dp": d}
    prv = {"frames": (f + 62) % 64, "dp": d}

    def remote(src, dst, ss, rs, to):
        return pltpu.make_async_remote_copy(
            src_ref=src, dst_ref=dst, send_sem=ss, recv_sem=rs, device_id=to, device_id_type=MESH
        )

    barrier = pltpu.get_barrier_semaphore()
    partners = [sib, nxt, prv]
    for yy, xx in ((yin, x), (y, xin), (yin, xin)):
        partners += [dev(z, yy, xx, 0), dev(z, yy, xx, 1)]
    for k in (2, 3):
        yy = (ycross, (y + 2) % 4)[k - 2]
        partners += [dev(z, yy, x, 0), dev(z, yy, x, 1)]
    for xx in (xcross, xop):
        partners += [dev(z, y, xx, 0), dev(z, y, xx, 1)]
    partners += [dev(zz, (y + dy) % 4, x, c) for zz in (zp, zm, zo) for dy in range(4)]
    for to in partners:
        pl.semaphore_signal(barrier, inc=1, device_id=to, device_id_type=MESH)

    x_local = pltpu.make_async_copy(x_hbm, x_ref, loc_sem.at[1])
    x_local.start()
    for h in range(2):
        wide = []
        for a in range(3):
            taps = [w_ref[:, (3 * a + b) * CH + h * HALF : (3 * a + b) * CH + (h + 1) * HALF].astype(f32) for b in range(3)]
            wide.append(jnp.concatenate(taps + [jnp.zeros((10, WIDE - 3 * HALF), f32)], axis=1))
        for half in range(2):
            pieces = [wide[a][:, lb * 128 : lb * 128 + 128] for lb in range(4 * half, 4 * half + 4) for a in range(3)]
            wpc[h, half] = jnp.concatenate(pieces + [jnp.zeros((8, 128), f32)], axis=0).astype(bf16)
    pl.semaphore_wait(barrier, len(partners))
    me8 = (y0 * 2 + xl) * 2 + c
    def p1_all(half):
        seven = p1.at[0:7, half]
        return remote(seven, seven, p1_s.at[half], p1_r.at[half], sib)

    p1c = ([], [])
    for half in range(2):
        k = 0
        for yy, xx, dc in ((yin, xin, 0), (yin, xin, 1), (yin, x, 0), (yin, x, 1), (y, xin, 0), (y, xin, 1), (y, x, 1)):
            cc = c + dc - 2 * c * dc
            to = dev(z, yy, xx, cc)
            p1c[half].append(remote(wpc.at[cc, half], p1.at[me8, half], p1_s.at[half], p1_r.at[half], to))
            k += 1
    for cp in p1c[0]:
        cp.start()
    interior = (pl.ds(c * 4, 4), pl.ds(16, 256))
    g_local = pltpu.make_async_copy(g_hbm, gp.at[interior], loc_sem.at[0])
    g_remote = remote(g_hbm, gp.at[interior], ex_s.at[0], ex_r.at[0], sib)
    g_local.start()
    p1[me8] = wpc[c]

    x_local.wait()
    def split(t, _):
        r = rows16(t * 256, 256)
        v = x_ref[r, :].astype(f32)
        xs[0, r, :HALF] = v[:, :HALF].astype(bf16)
        xs[1, r, :HALF] = v[:, HALF:].astype(bf16)
        return 0

    lax.fori_loop(0, 4, split, 0)
    x_remote = remote(xs.at[oc], xb, ex_s.at[1], ex_r.at[1], sib)
    x_remote.start()
    g_remote.start()

    def read_x(t):
        r = rows16((t % 4) * 256, 256)
        mine = xs[c, r, :HALF]
        other = xb[r, :HALF]
        return jnp.where(t // 4 == c, mine, other).astype(f32)

    zero16 = jnp.zeros((16, CH), bf16)
    zero16w = jnp.zeros((16, WIDE), bf16)
    for t in range(8):
        gp[t, 0:16, :] = zero16
        gp[t, 272:288, :] = zero16
        ap[t, 0:16, :] = zero16w
        ap[t, 272:288, :] = zero16w

    oi = lax.broadcasted_iota(jnp.int32, (CH, CH), 0)
    li = lax.broadcasted_iota(jnp.int32, (CH, CH), 1)
    q = (oi >= HALF).astype(jnp.int32)
    rr = oi - HALF * q
    zy = div20(rr)
    src_row = (2 * zy + (q + xl - 2 * q * xl)) * 20 + (rr - 20 * zy)
    pm[...] = (li == src_row).astype(f32).astype(bf16)
    gi = div20(lax.broadcasted_iota(jnp.int32, (HALF, HALF), 0))
    gj = div20(lax.broadcasted_iota(jnp.int32, (HALF, HALF), 1))
    group_mean = jnp.where(gi == gj, 1.0 / 5120.0, 0.0).astype(f32)

    def spread_groups(v):
        return jnp.dot(v, group_mean, preferred_element_type=f32, precision=HIGH)

    mine0 = c == 0
    gain_all, bias_all = gain_ref[...].reshape(1, CH), bias_ref[...].reshape(1, CH)
    gain = jnp.where(mine0, gain_all[:, :HALF], gain_all[:, HALF:])
    bias = jnp.where(mine0, bias_all[:, :HALF], bias_all[:, HALF:])

    def transpose(t):
        gt[:, pl.ds(pl.multiple_of(t * 256, 256), 256)] = dot_nt(pm[...], gp[t, 16:272, :]).astype(bf16)

    g_local.wait()

    def transpose_mine(i, _):
        transpose(c * 4 + i)
        return 0

    lax.fori_loop(0, 4, transpose_mine, 0)
    for cp in p1c[1]:
        cp.start()

    x_remote.wait_recv()

    def stat_sum(t, _):
        s1[pl.ds(t, 1), :] = jnp.sum(read_x(t), axis=0, keepdims=True)
        return 0

    lax.fori_loop(0, 8, stat_sum, 0)
    cen[...] = spread_groups(s1[...])

    def stat_sq(t, _):
        v = read_x(t) - cen[pl.ds(t, 1), :]
        s2[pl.ds(t, 1), :] = jnp.sum(v * v, axis=0, keepdims=True)
        return 0

    lax.fori_loop(0, 8, stat_sq, 0)
    inv[...] = lax.rsqrt(spread_groups(s2[...]) + EPS)

    blk = z * 2 + y1

    def dense(half):
        p1_all(half).wait_recv()
        for lb in range(4):
            for a in range(3):
                r = (lb * 3 + a) * 10
                piece = jnp.concatenate([p1[s, half, r : r + 10, :].astype(f32) for s in range(8)], axis=0)
                at = (half * 4 + lb) * 128
                w[a, blk, :, at : at + 128] = piece.astype(bf16)

    dense(0)

    def lanes(qq, n=256):
        return pl.ds(pl.multiple_of(qq * 256, 256), n)

    def wsl(b, qq):
        return w.at[:, b, :, lanes(qq)]

    def quarter(j):
        return (2 * (j % 2) + 1 - y0) if j < 2 else (2 * (j % 2) + y0)

    def z_own(k, j):
        s = wsl(blk, quarter(j))
        return remote(s, s, zo_s.at[0], zo_r.at[j], dev((zp, zm)[k], y, x, c))

    def z_fwd(j):
        up = j % 2 == 0
        s = wsl((zm if up else zp) * 2 + y1, quarter(j))
        return remote(s, s, zf_s.at[0], zf_r.at[j], dev(zp if up else zm, y, x, c))

    zrel = (z, zm, zp, zo)

    def cross(k, h):
        s = wsl(zrel[k] * 2 + y1, 2 * h + 1 - y0)
        return remote(s, s, cr_s.at[0], cr_r.at[k, h], dev(z, ycross, x, c))

    def inner(k, h):
        s = wsl(zrel[k] * 2 + 1 - y1, 2 * h + y0)
        return remote(s, s, yi_s.at[0], yi_r.at[h], dev(z, yin, x, c))

    def inner_all(h):
        one = w.at[:, 0]
        return remote(one, one, yi_s.at[0], yi_r.at[h], sib)

    def z_start(j):
        z_own(0, j).start()
        z_own(1, j).start()

    def z_wait(j):
        two = w.at[:, 0:2, :, 0:256]
        remote(two, two, zo_s.at[0], zo_r.at[j], sib).wait_recv()

    def hook_in(k, h):
        cross(k, h).wait_recv()
        inner(k, h).start()

    def hook0():
        dense(1)
        z_start(1)
        cross(0, 1).start()

    def hook1():
        z_wait(0)
        z_fwd(0).start()
        cross(1, 0).start()
        hook_in(0, 0)
        z_start(2)

    def hook2():
        cross(2, 0).start()

    def hook3():
        z_wait(1)
        z_fwd(1).start()
        hook_in(0, 1)
        z_start(3)

    def hook4():
        z_fwd(0).wait_recv()
        cross(3, 0).start()
        hook_in(1, 0)

    def hook5():
        cross(1, 1).start()
        z_wait(2)
        z_fwd(2).start()

    def hook6():
        hook_in(2, 0)
        z_fwd(1).wait_recv()
        cross(2, 1).start()

    def hook7():
        hook_in(3, 0)
        cross(3, 1).start()

    def hook8():
        hook_in(1, 1)
        z_wait(3)
        z_fwd(3).start()

    cross(0, 0).start()
    z_start(0)

    col = lax.broadcasted_iota(jnp.int32, (256, HALF), 0) % 16

    def normed_of(t):
        return (read_x(t) - cen[pl.ds(t, 1), :]) * inv[pl.ds(t, 1), :]

    def forward(t, _):
        before = normed_of(t) * gain + bias
        act = before / (1.0 + jnp.exp(-before))
        left = jnp.where(col == 0, 0.0, pltpu.roll(act, 1, 0))
        right = jnp.where(col == 15, 0.0, pltpu.roll(act, 255, 0))
        cat = jnp.concatenate([left, act, right, jnp.zeros((256, WIDE - 3 * HALF), f32)], axis=1)
        ap[t, 16:272, :] = cat.astype(bf16)
        return 0

    g_remote.wait_recv()

    def forward_pair(i, _):
        transpose(oc * 4 + i)
        forward(2 * i, 0)
        forward(2 * i + 1, 0)
        pl.when(i == 1)(hook0)
        return 0

    lax.fori_loop(0, 4, forward_pair, 0)
    hook1()

    def x_copy(i, k):
        to = (xin, xcross)[k]
        return remote(wgs.at[i, k], xr.at[i, k], x_s.at[0], x_r.at[i], dev(z, y, to, c))

    def x_all(i):
        return remote(wgs.at[i], xr.at[i], x_s.at[0], x_r.at[i], sib)

    def wg_step(i, _):
        a, n = i // 2, i % 2
        cols = pl.ds(pl.multiple_of(n * 512, 512), 512)
        acc = None
        for t in range(8):
            v = dot(gt[:, t * 256 : t * 256 + 256], ap[t, rows16(a * 16, 256), cols])
            acc = v if acc is None else acc + v
        s_buf[i] = acc[:HALF, :]
        wgs[i, 0] = acc[HALF:, :256].astype(bf16)
        wgs[i, 1] = acc[HALF:, 256:].astype(bf16)
        x_copy(i, 0).start()
        x_copy(i, 1).start()

        for k, hook in enumerate((hook2, hook3, hook4, hook5, hook6, hook7)):
            pl.when(i == k)(hook)
        pl.when(i == 4)(lambda: stage1(0))
        return 0

    def z1_copy(i, k):
        return remote(z1s.at[i, k], z1r.at[i, k], z1_ss.at[0], z1_rs.at[i], dev((zp, zm)[k], y, x, c))

    def z1_all(i):
        return remote(z1s.at[i], z1r.at[i], z1_ss.at[0], z1_rs.at[i], sib)

    def z2_copy(i, k):
        return remote(z2s.at[i, k], z2r.at[i, k], z2_ss.at[0], z2_rs.at[i], dev((zp, zm)[k], y, x, c))

    def z2_all(i):
        return remote(z2s.at[i], z2r.at[i], z2_ss.at[0], z2_rs.at[i], sib)

    def y_copy(i, r):
        dy, dc = r // 2, r % 2
        yy, cc = (y + dy) % 4, c + dc - 2 * c * dc
        return remote(ys.at[i, yy * 2 + cc], yr.at[i, r], y_ss.at[0], y_rs.at[i], dev(z, yy, x, cc))

    def y_all(i):
        seven = yr.at[i, 1:8]
        return remote(seven, seven, y_ss.at[0], y_rs.at[i], sib)

    def d_copy(i):
        return remote(ds_.at[i], dr.at[i], d_ss.at[0], d_rs.at[0], dev(z, y, xop, c))

    def block(b):
        return rows16(b * 80, 80)

    def stage1(i):
        x_all(i).wait_recv()
        s_buf[i, :, :256] = s_buf[i, :, :256] + xr[i, 0].astype(f32)
        s_buf[i, :, 256:] = s_buf[i, :, 256:] + xr[i, 1].astype(f32)
        z1s[i, 0] = s_buf[i, block(zo), 0:256].astype(bf16)
        z1s[i, 1] = s_buf[i, block(zo), 256:512].astype(bf16)
        z1_copy(i, 0).start()
        z1_copy(i, 1).start()

    def relay(i):
        z1_all(i).wait_recv()
        z2s[i, 0, :, 0:256] = (s_buf[i, block(zp), 0:256] + z1r[i, 0].astype(f32)).astype(bf16)
        z2s[i, 0, :, 256:512] = s_buf[i, block(zp), 256:512].astype(bf16)
        z2_copy(i, 0).start()
        z2s[i, 1, :, 0:256] = s_buf[i, block(zm), 0:256].astype(bf16)
        z2s[i, 1, :, 256:512] = (s_buf[i, block(zm), 256:512] + z1r[i, 1].astype(f32)).astype(bf16)
        z2_copy(i, 1).start()

    def stage2(i):
        z2_all(i).wait_recv()
        total = s_buf[i, block(z), :] + z2r[i, 0].astype(f32) + z2r[i, 1].astype(f32)
        total = jnp.concatenate([total, jnp.zeros((8, 512), f32)], axis=0)
        for k in range(8):
            piece = total[10 * k : 10 * k + 16, :]
            yf[i, k] = piece
            ys[i, k] = piece.astype(bf16)
        for r in range(1, 8):
            y_copy(i, r).start()

    def stage3(i):
        y_all(i).wait_recv()
        own = yf[i, y * 2 + c]
        for dy in (1, 2, 3):
            own = own + yr[i, 2 * dy].astype(f32)
        other = yr[i, 1].astype(f32)
        for dy in (1, 2, 3):
            other = other + yr[i, 2 * dy + 1].astype(f32)
        ds_[i, 0] = own
        ds_[i, 1] = other
        d_copy(i).start()

    def stage4(i):
        own = (ds_[i, 0] + dr[i, 0]) * scale
        other = (ds_[i, 1] + dr[i, 1]) * scale
        a, n = i // 2, i % 2
        cols = pl.ds(pl.multiple_of(n * 512, 512), 512)
        fin[0, a, :, cols] = jnp.where(mine0, own, other)
        fin[1, a, :, cols] = jnp.where(mine0, other, own)

    lax.fori_loop(0, 6, wg_step, 0)
    stage1(1)
    relay(0)
    hook8()
    inner_all(0).wait_recv()
    z_fwd(2).wait_recv()

    def back1(t, _):
        r = rows16(t * 256, 256)
        v = y_acc[r, :]
        right = jnp.where(col == 15, 0.0, pltpu.roll(v[:, :HALF], 255, 0))
        left = jnp.where(col == 0, 0.0, pltpu.roll(v[:, 2 * HALF : 3 * HALF], 1, 0))
        act_grad = right + v[:, HALF : 2 * HALF] + left
        normed = normed_of(t)
        before = normed * gain + bias
        g = 1.0 / (1.0 + jnp.exp(-before))
        p = act_grad * g * (1.0 + before * (1.0 - g))
        pre[r, :] = p
        s1[pl.ds(t, 1), :] = jnp.sum(p * normed, axis=0, keepdims=True)
        s2[pl.ds(t, 1), :] = jnp.sum(p, axis=0, keepdims=True)
        return 0

    def back2(t, _):
        r = rows16(t * 256, 256)
        v = pre[r, :] * gain - m1[pl.ds(t, 1), :] - normed_of(t) * m2[pl.ds(t, 1), :]
        sgp[t + 1] = (v * inv[pl.ds(t, 1), :]).astype(bf16)
        return 0

    def back1_of(frames):
        for t in frames:
            back1(t, 0)

    def group_terms():
        both = spread_groups(jnp.concatenate([s2[...] * gain, s1[...] * gain], axis=0))
        m1[...] = both[0:8]
        m2[...] = both[8:16]

    halo = [
        remote(hs.at[0], hr.at[0], h_ss.at[0], h_rs.at[0], nxt),
        remote(hs.at[1], hr.at[1], h_ss.at[1], h_rs.at[1], prv),
    ]
    ch_id = lax.broadcasted_iota(jnp.int32, (HALF, 80), 0) + c * HALF
    selm[0] = (ch_id == bwd_ref[...].reshape(1, 80)).astype(f32).astype(bf16)
    selm[1] = (ch_id == fwd_ref[...].reshape(1, 80)).astype(f32).astype(bf16)

    def edge_frames():
        group_terms()
        back2(0, 0)
        back2(7, 0)
        hs[0, :, :80] = dot(sgp[8], selm[0]).astype(bf16)
        hs[1, :, :80] = dot(sgp[1], selm[1]).astype(bf16)
        halo[0].start()
        halo[1].start()

    def act_dot(n, tt):
        cols = pl.ds(n * 512, 512)
        lhs = jnp.concatenate(
            [
                jnp.concatenate([gp[tt * 2 + t, 16 * (2 - a) : 16 * (2 - a) + 256, :] for a in range(3)], axis=1)
                for t in range(2)
            ],
            axis=0,
        )
        rhs = w[:, :, :, cols].reshape(3 * CH, 512)
        y_acc[rows16(tt * 512, 512), cols] = dot(lhs, rhs)

    def act_step(i, _):
        act_dot(0, i)
        plan = {
            0: [(stage1, 2), (relay, 1)],
            1: [(stage2, 0)],
            2: [(stage1, 3)],
            3: [(relay, 2), (stage2, 1)],
        }
        for k in range(4):

            @pl.when(i == k)
            def _(k=k):
                if k == 0:
                    hook_in(2, 1)
                for stage, chunk in plan.get(k, []):
                    stage(chunk)
                if k == 1:
                    hook_in(3, 1)

        return 0

    lax.fori_loop(0, 4, act_step, 0)
    stage1(4)
    inner_all(1).wait_recv()
    z_fwd(3).wait_recv()
    act_dot(1, 3)
    stage1(5)
    relay(3)
    act_dot(1, 0)
    back1_of((6, 7))
    relay(4)
    stage2(2)
    act_dot(1, 1)
    back1_of((0, 1))
    stage3(0)
    edge_frames()
    relay(5)
    act_dot(1, 2)
    stage2(3)
    back1_of((2, 3))
    stage3(1)

    def a1_copy(r):
        dx, dc = r // 2, r % 2
        cc = c + dc - 2 * c * dc
        return remote(a1s, a1r.at[r], a1_ss.at[0], a1_rs.at[0], dev(z, y, (x + dx) % 4, cc))

    def a2_copy(r):
        return remote(a2s, a2r.at[r], a2_ss.at[0], a2_rs.at[0], dev((z + r // 4) % 4, (y + r % 4) % 4, x, c))

    a1_all = remote(a1r.at[1:8], a1r.at[1:8], a1_ss.at[0], a1_rs.at[0], sib)
    a2_all = remote(a2r.at[1:16], a2r.at[1:16], a2_ss.at[0], a2_rs.at[0], sib)

    back1_of((4, 5))
    total = [jnp.sum(v[...], axis=0, keepdims=True) for v in (s1, s2)]
    a1s[:, :HALF] = jnp.concatenate(total + [jnp.zeros((6, HALF), f32)], axis=0)
    for r in range(1, 8):
        a1_copy(r).start()
    stage2(4)
    group_terms()
    lax.fori_loop(1, 7, back2, 0)
    ones = jnp.ones((8, 80), bf16)
    bwd_mask = dot_nt(ones, selm[0])[0:1, :] > 0.5
    fwd_mask = dot_nt(ones, selm[1])[0:1, :] > 0.5

    def shift(t):
        v = jnp.where(bwd_mask, sgp[t].astype(f32), sgp[t + 1].astype(f32))
        return jnp.where(fwd_mask, sgp[t + 2].astype(f32), v)

    def shift_other(i, _):
        igs[i, :, :HALF] = shift(oc * 4 + i).astype(bf16)
        return 0

    lax.fori_loop(c, c + 3, shift_other, 0)
    inside = pl.ds(c, 3)
    i_copies = [
        remote(igs.at[inside], igr.at[inside], ex_s.at[2], ex_r.at[2], sib),
        remote(igs.at[3 * oc], igr.at[3 * oc], ex_s.at[3], ex_r.at[3], sib),
    ]
    i_copies[0].start()
    stage2(5)
    stage3(2)
    halo[0].wait_recv()
    halo[1].wait_recv()
    keep_prev = jnp.where(f >= 2, 1.0, 0.0)
    keep_next = jnp.where(f < 62, 1.0, 0.0)
    sgp[0] = (dot_nt(hr[0, :, :80], selm[0]) * keep_prev).astype(bf16)
    sgp[9] = (dot_nt(hr[1, :, :80], selm[1]) * keep_next).astype(bf16)
    shift_other(3 * oc, 0)
    i_copies[1].start()
    a1_all.wait_recv()
    own = a1s[0:2, :HALF]
    for r in (2, 4, 6):
        own = own + a1r[r, 0:2, :HALF]
    other = a1r[1, 0:2, :HALF]
    for r in (3, 5, 7):
        other = other + a1r[r, 0:2, :HALF]
    a2s[:, :HALF] = jnp.concatenate([own, other, jnp.zeros((4, HALF), f32)], axis=0)
    for r in range(1, 16):
        a2_copy(r).start()
    stage3(3)
    stage3(4)
    stage3(5)
    inner_frames = igr.at[0:3]
    remote(inner_frames, inner_frames, ex_s.at[2], ex_r.at[2], sib).wait_recv()
    i_copies[1].wait_recv()

    def assemble(i, _):
        own = shift(c * 4 + i)
        other = igr[i, :, :HALF].astype(f32)
        v = jnp.concatenate([jnp.where(mine0, own, other), jnp.where(mine0, other, own)], axis=1)
        igo[rows16(i * 256, 256), :] = v.astype(bf16)
        return 0

    lax.fori_loop(0, 4, assemble, 0)
    o_copy = pltpu.make_async_copy(igo, ig_hbm, loc_sem.at[2])
    o_copy.start()

    p1_all(0).wait_send()
    p1_all(1).wait_send()
    for cp in (g_remote, x_remote, *i_copies, halo[0], halo[1]):
        cp.wait_send()
    one, two = w.at[:, 0], w.at[:, 0:2]
    for ref, sem in ((two, zo_s), (one, zf_s), (two, cr_s), (two, yi_s), (wgs, x_s), (z1s, z1_ss), (z2s, z2_ss), (yr.at[:, 1:8], y_ss)):
        remote(ref, ref, sem.at[0], sem.at[0], sib).wait_send()
    a1_all.wait_send()

    remote(ds_, dr, d_ss.at[0], d_rs.at[0], sib).wait_recv()
    for i in range(6):
        stage4(i)
    for a in range(3):
        for b in range(3):
            tap = jnp.concatenate([fin[h, a, 0:10, b * HALF : (b + 1) * HALF] for h in range(2)], axis=1)
            wg_ref[:, (3 * a + b) * CH : (3 * a + b + 1) * CH] = tap
    total = a2s[:, :HALF]
    a2_all.wait_recv()
    for r in range(1, 16):
        total = total + a2r[r, :, :HALF]
    total = total * scale
    own, other = total[0:2, :], total[2:4, :]
    both = jnp.concatenate([jnp.where(mine0, own, other), jnp.where(mine0, other, own)], axis=1)
    gg_ref[...] = both[0:1, :].reshape(CH)
    bg_ref[...] = both[1:2, :].reshape(CH)
    a2_all.wait_send()
    remote(ds_, dr, d_ss.at[0], d_rs.at[0], sib).wait_send()
    o_copy.wait()


def hand_over(ig_in, wg_in, gg_in, bg_in, ig_out, wg_out, gg_out, bg_out, ig, wg, gg, bg, in_sem, out_sem):
    rows = [pl.ds(256 * k, 256) for k in range(4)]
    sets = [(ig_in.at[r], ig.at[r], ig_out.at[r]) for r in rows]
    sets += [(wg_in, wg, wg_out), (gg_in, gg, gg_out), (bg_in, bg, bg_out)]
    first = [pltpu.make_async_copy(a, b, in_sem.at[k]) for k, (a, b, _) in enumerate(sets)]
    second = [pltpu.make_async_copy(b, d, out_sem.at[k]) for k, (_, b, d) in enumerate(sets)]
    for cp in first:
        cp.start()
    for a, b in zip(first, second):
        a.wait()
        b.start()
    for cp in second:
        cp.wait()


def on_device(shifted, out_grad, conv_weight, norm_gain, norm_bias, shift_fwd, shift_bwd):
    scale = 131072.0 ** (-0.5)
    x = shifted.reshape(1024, CH)
    g = out_grad.reshape(4, 256, CH)
    dma = pltpu.SemaphoreType.DMA
    vm = pltpu.VMEM
    scratch = [
        vm((2, 2, 128, 128), bf16), vm((2, 3, 16, WIDE), f32), vm((1024, CH), bf16),
        vm((2, 1024, FULL), bf16), vm((1024, FULL), bf16), vm((8, 288, CH), bf16), vm((CH, 2048), bf16),
        vm((CH, CH), bf16), vm((8, 288, WIDE), bf16), vm((8, 2, 128, 128), bf16), vm((3, 8, 80, WIDE), bf16),
        vm((2048, WIDE), f32), vm((2048, HALF), f32),
        vm((8, HALF), f32), vm((8, HALF), f32), vm((8, HALF), f32), vm((8, HALF), f32), vm((8, HALF), f32), vm((8, HALF), f32),
        vm((6, HALF, 512), f32), vm((6, 2, HALF, 256), bf16), vm((6, 2, HALF, 256), bf16),
        vm((6, 2, 80, 256), bf16), vm((6, 2, 80, 256), bf16), vm((6, 2, 80, 512), bf16), vm((6, 2, 80, 512), bf16),
        vm((6, 8, 16, 512), f32), vm((6, 8, 16, 512), bf16), vm((6, 8, 16, 512), bf16),
        vm((6, 2, 16, 512), f32), vm((6, 2, 16, 512), f32),
        vm((10, 256, HALF), bf16), vm((4, 256, FULL), bf16), vm((4, 256, FULL), bf16), vm((1024, CH), bf16),
        vm((2, 256, 128), bf16), vm((2, 256, 128), bf16), vm((2, HALF, 80), bf16),
        vm((8, FULL), f32), vm((8, 8, FULL), f32), vm((8, FULL), f32), vm((16, 8, FULL), f32),
        dma((4,)), dma((4,)), dma((4,)), dma((2,)), dma((2,)), dma((1,)), dma((4,)), dma((1,)), dma((4,)),
        dma((1,)), dma((4, 2)), dma((1,)), dma((2,)),
        dma((1,)), dma((6,)), dma((1,)), dma((6,)), dma((1,)), dma((6,)), dma((1,)), dma((6,)),
        dma((1,)), dma((1,)), dma((2,)), dma((2,)), dma((1,)), dma((1,)), dma((1,)), dma((1,)),
    ]
    v = pl.BlockSpec(memory_space=pltpu.VMEM)

    def body(*refs):
        kernel(scale, *refs)

    shapes = (
        jax.ShapeDtypeStruct((1024, CH), bf16),
        jax.ShapeDtypeStruct((10, 9 * CH), f32),
        jax.ShapeDtypeStruct((CH,), f32),
        jax.ShapeDtypeStruct((CH,), f32),
    )
    anywhere = pl.BlockSpec(memory_space=pl.ANY)
    parts = pl.pallas_call(
        body,
        out_shape=shapes,
        in_specs=[pl.BlockSpec(memory_space=pl.ANY), pl.BlockSpec(memory_space=pl.ANY), v, v, v, v, v],
        out_specs=(anywhere, v, v, v),
        scratch_shapes=scratch,
        compiler_params=pltpu.CompilerParams(collective_id=0, has_side_effects=True, vmem_limit_bytes=60 << 20),
    )(x, g, conv_weight, norm_gain, norm_bias, shift_fwd, shift_bwd)
    ig, wg, gg, bg = pl.pallas_call(
        hand_over,
        out_shape=shapes,
        in_specs=[anywhere] * 4,
        out_specs=(anywhere,) * 4,
        scratch_shapes=[
            vm((1024, CH), bf16), vm((10, 9 * CH), f32), vm((CH,), f32), vm((CH,), f32), dma((7,)), dma((7,)),
        ],
    )(*parts)
    return (ig.reshape(shifted.shape), wg, gg, bg)


def solution(mesh):
    in_specs = (
        P("dp", "frames", None, None, None),
        P("dp", "frames", None, None, None),
        P("frames", None),
        P(),
        P(),
        P(),
        P(),
    )
    out_specs = (P("dp", "frames", None, None, None), P("frames", None), P(), P())
    return jax.shard_map(
        on_device, mesh=mesh, in_specs=in_specs, out_specs=out_specs, check_vma=False
    )
```
